256 devices in a mesh: dp: 128 (over x, z, y), mp: 2 (over core).
Axes of the slice: x: 4, y: 4, z: 8, core: 2. Of those that a mesh axis runs over, the one named last changes fastest.
Arguments:
- queries: float32 [32768, 4096], P('dp', 'mp'), may hold values from -5 to 5
- passages: float32 [32768, 4096], P('dp', 'mp'), may hold values from -5 to 5
- cluster_of_block: int32 [128], replicated, may hold values from 0 to 63, never falling along the last dimension, each value on 1 to 4 neighbouring positions
- positive_row: int32 [32768], P('dp'), may hold values from 0 to 255
- query_weight: float32 [32768], P('dp'), may hold values from 0.3 to 3
Outputs:
- mean_loss: float32 [], replicated
- query_grad: float32 [32768, 4096], P('dp', 'mp')
- passage_grad: float32 [32768, 4096], P('dp', 'mp')
The draws below stay inside these ranges and needn't reach their ends.
Inputs may be any that keep to these rules, and one draw needn't show every extreme that they name: `cluster_of_block`: never falls from one block to the next; every cluster covers 1 to 4 consecutive blocks, one exactly 4.
All inputs are finite; a program needn't handle non-finite values.
Results may differ from the reference program's by a relative error of at most 0.0051.
Values may be sent and summed in bfloat16 or wider, within the bound.
A program may use at most 128 MiB of HBM per device.

```python
import math
import jax
import jax.numpy as jnp
import numpy as np
from jax import lax

D = 4096
BLK = 256
CMAX = 4
NB = 128
NQ = 32768
N_DP = 128


def shared_rows(key, limit):
    return jnp.clip(jax.random.normal(jax.random.fold_in(key, 5), (NQ, D), jnp.float32), -limit, limit)


def draw_passages(key, part):
    return shared_rows(key, 5.0)


def draw_queries(key, part):
    own_key = jax.random.fold_in(key, 22)
    return jnp.clip(jax.random.normal(own_key, (NQ, D), jnp.float32), -5.0, 5.0)


def touch_ends(drawn, key, smallest, largest):
    longest = drawn.shape.index(max(drawn.shape))
    spots = []
    for shift in (0, 1):
        where = [jax.random.randint(jax.random.fold_in(key, axis), (), 0, length) for axis, length in enumerate(drawn.shape)]
        where[longest] = (where[longest] + shift) % drawn.shape[longest]
        spots.append(tuple(where))
    return drawn.at[spots[0]].set(smallest).at[spots[1]].set(largest)


def block_levels(rng, dims, split, least, high):
    def one(dim, shards_of):
        draws = jax.random.uniform(jax.random.fold_in(jax.random.fold_in(rng, 6), dim), (shards_of,), jnp.float32, least / len(split), high / len(split))
        return jnp.repeat(jnp.exp(draws), dims[dim] // shards_of).reshape((-1,) + (1,) * (len(dims) - dim - 1))

    factor_of = one(*split[0])
    for cut in split[1:]:
        factor_of = factor_of * one(*cut)
    return factor_of


def profile(count, total, most, slope):
    loads = [(1 << 20) // math.isqrt(rank ** slope) + 1 for rank in range(2, count + 1)]
    rest, holding = total - most - (count - 1), [1] * (count - 1)
    while rest > 0:
        candidates = [i for i in range(count - 1) if holding[i] < most]
        whole, remaining = sum([loads[i] for i in candidates]), rest
        for i in candidates:
            extra = min(most - holding[i], max(1, remaining * loads[i] // whole), rest)
            holding[i] = holding[i] + extra
            rest = rest - extra
    return np.array([most] + holding)


def ragged(stream_key, number_of, total, most, skew):
    if number_of == 2:
        one = jax.random.randint(stream_key, (), max(1, total - most), min(most, total - 1) + 1)
        return jnp.stack([one, total - one])
    sizes = jnp.asarray(profile(number_of, total, most, skew), jnp.int32)
    couples = (number_of - 1) // 2
    source_of, receiver = sizes[1:1 + 2 * couples:2], sizes[2:2 + 2 * couples:2]
    room = jnp.minimum(source_of - 1, most - receiver)
    moved = jax.random.randint(jax.random.fold_in(stream_key, 1), (couples,), 0, 1 << 20) % (room + 1)
    sizes = sizes.at[1:1 + 2 * couples:2].set(source_of - moved).at[2:2 + 2 * couples:2].set(receiver + moved)
    return sizes[jax.random.permutation(jax.random.fold_in(stream_key, 2), number_of)]


def setup_inputs(seed: int = 0) -> dict:
    arg_keys = jax.random.split(jax.random.key(seed), 6)
    queries = draw_queries(jax.random.fold_in(arg_keys[5], 71), 0)
    passages = draw_passages(jax.random.fold_in(arg_keys[5], 71), 0)
    cluster_of_block = jnp.searchsorted(jnp.cumsum(ragged(arg_keys[2], N_DP // 2, NB, CMAX, 2)), jnp.arange(NB), side="right").astype(jnp.int32)
    positive_row = touch_ends(jax.random.randint(arg_keys[3], (NQ,), 0, BLK), jax.random.fold_in(arg_keys[3], 1), 0, BLK - 1).astype(jnp.int32)
    query_weight = jnp.clip(jnp.exp(math.log(3.0) - 2.3025851 * jax.random.uniform(arg_keys[4], (NQ,), jnp.float32) ** block_levels(arg_keys[4], (NQ,), ((0, 128),), -0.2, 0.2)), 0.3, 3.0)
    return dict(queries=queries, passages=passages, cluster_of_block=cluster_of_block, positive_row=positive_row, query_weight=query_weight)


def tile_dot(left_tile, right_tile):
    return lax.dot_general(left_tile, right_tile, (((1,), (1,)), ((), ())), preferred_element_type=jnp.float32)

def tile_back(coeff_tile, query_tile):
    return lax.dot_general(coeff_tile, query_tile, (((0,), (0,)), ((), ())), preferred_element_type=jnp.float32)

def reference(queries, passages, cluster_of_block, positive_row, query_weight):
    reach = CMAX - 1
    score_scale = 3.0 / math.sqrt(D)
    query_blocks = queries.astype(jnp.bfloat16).reshape(NB, BLK, D)
    passage_blocks = passages.astype(jnp.bfloat16).reshape(NB, BLK, D)
    padding = jnp.zeros((reach, BLK, D), jnp.bfloat16)
    padded = jnp.concatenate([padding, passage_blocks, padding], 0)
    edge_ids = jnp.full((reach,), -1, jnp.int32)
    cluster_pad = jnp.concatenate([edge_ids, cluster_of_block.astype(jnp.int32), edge_ids], 0)
    positives = positive_row.astype(jnp.int32).reshape(NB, BLK)
    weights = query_weight.reshape(NB, BLK)
    column_ids = jnp.arange(BLK, dtype=jnp.int32)
    zero_scores = jnp.zeros((BLK, BLK), jnp.float32)
    zero_rows = jnp.zeros((BLK, D), jnp.float32)

    def visit(carry, index):
        grad_pad, loss_sum = carry
        query_tile = lax.dynamic_index_in_dim(query_blocks, index, 0, keepdims=False)
        own_cluster = lax.dynamic_index_in_dim(cluster_pad, index + reach, 0, keepdims=False)
        block_weight = lax.dynamic_index_in_dim(weights, index, 0, keepdims=False)
        block_pos = lax.dynamic_index_in_dim(positives, index, 0, keepdims=False)
        tiles = []
        flags = []
        partial_value = []
        for offset in range(-reach, reach + 1):
            place = index + reach + offset
            passage_tile = lax.dynamic_index_in_dim(padded, place, 0, keepdims=False)
            linked_flag = lax.dynamic_index_in_dim(cluster_pad, place, 0, keepdims=False) == own_cluster
            partial_value.append(lax.cond(linked_flag, lambda other: tile_dot(query_tile, other), lambda other: zero_scores, passage_tile))
            tiles.append(passage_tile)
            flags.append(linked_flag)
        valid = jnp.stack(flags)
        masked = jnp.where(valid[:, None, None], jnp.stack(partial_value) * score_scale, -1e+30)
        row_max = lax.optimization_barrier(jnp.max(masked, axis=(0, 2)))
        expo = jnp.exp(masked - row_max[None, :, None])
        row_total = lax.optimization_barrier(jnp.sum(expo, axis=(0, 2)))
        positive_hit = block_pos[:, None] == column_ids[None, :]
        picked = lax.optimization_barrier(jnp.sum(jnp.where(positive_hit, masked[reach], 0.0), axis=1))
        loss_rows = row_max + jnp.log(row_total) - picked
        weighted = block_weight[None, :, None] * (expo / row_total[None, :, None])
        own_term = weighted[reach] - jnp.where(positive_hit, block_weight[:, None], 0.0)
        weighted = jnp.concatenate([weighted[:reach], own_term[None], weighted[reach + 1:]], 0)
        coeff = weighted.astype(jnp.bfloat16)
        query_grad = zero_rows
        for slot in range(2 * reach + 1):
            query_grad = query_grad + lax.cond(flags[slot], lambda coeff_tile, other: jnp.dot(coeff_tile, other, preferred_element_type=jnp.float32), lambda coeff_tile, other: zero_rows, coeff[slot], tiles[slot])
            grad_term = lax.cond(flags[slot], lambda coeff_tile: tile_back(coeff_tile, query_tile), lambda coeff_tile: zero_rows, coeff[slot])
            place = index + slot
            current = lax.dynamic_index_in_dim(grad_pad, place, 0, keepdims=False)
            grad_pad = lax.dynamic_update_index_in_dim(grad_pad, current + grad_term, place, 0)
        return ((grad_pad, loss_sum + jnp.sum(block_weight * loss_rows)), query_grad)
    start = (jnp.zeros((NB + 2 * reach, BLK, D), jnp.float32), jnp.zeros((), jnp.float32))
    (grad_pad, loss_sum), query_grads = lax.scan(visit, start, jnp.arange(NB, dtype=jnp.int32))
    passage_grad = grad_pad[reach:reach + NB].reshape(NQ, D)
    return (loss_sum / NQ, query_grads.reshape(NQ, D), passage_grad)
```

```python
import functools
import math

import jax
import jax.numpy as jnp
from jax import lax
from jax.experimental import pallas as pl
from jax.experimental.pallas import tpu as pltpu
from jax.sharding import PartitionSpec as P

MESH = pl.DeviceIdType.MESH
NY, NZ, NX = 4, 8, 4
CHUNK = 256
GROUP = 32


def nt_dot(left, right):
    return lax.dot_general(left, right, (((1,), (1,)), ((), ())), preferred_element_type=jnp.float32)


def nn_dot(left, right):
    return jnp.dot(left, right, preferred_element_type=jnp.float32)


def kernel(
    query_hbm, passage_hbm, cluster, positive, weight,
    loss_ref, query_grad_hbm, passage_grad_hbm,
    fresh, own, beside, staged, gathered,
    score_own, score_other, coeff, coeff_out, coeff_beside, coeff_staged, coeff_got, coeff_fwd, coeff_t,
    pos_cols, weight_cols, query_grad, passage_grad, loss_tile, loss_y, loss_z, loss_x,
    in_sem, z_send, z_recv, y_send, y_recv, s_send, s_recv,
    cz_send, cz_recv, cy_send, cy_recv, cf_send, cf_recv,
    ly_send, ly_recv, lz_send, lz_recv, lx_send, lx_recv, qg_sem, pg_sem,
):
    rows, width = query_hbm.shape
    count = width // CHUNK
    half = rows // 2
    planes = NX * NZ
    me = lax.axis_index("dp")
    core = lax.axis_index("mp")
    y = me % NY
    plane = me // NY
    z = plane % NZ
    x = plane // NZ

    def at_y(step):
        return plane * NY + (y + step) % NY

    def at_z(step):
        return (x * NZ + (z + step) % NZ) * NY + y

    def at_x(step):
        return (((x + step) % NX) * NZ + z) * NY + y

    left_plane = ((plane + planes - 1) % planes) * NY + y
    right_plane = ((plane + 1) % planes) * NY + y

    def arriving(k):
        start = pl.multiple_of(k * CHUNK, CHUNK)
        return pltpu.make_async_copy(passage_hbm.at[:, pl.ds(start, CHUNK)], fresh.at[k], in_sem.at[k])

    def arriving_query(k):
        start = pl.multiple_of(k * CHUNK, CHUNK)
        return pltpu.make_async_copy(
            query_hbm.at[:, pl.ds(start, CHUNK)], fresh.at[count + k], in_sem.at[count + k]
        )

    def start_in(k, carry):
        arriving(k).start()
        return carry

    def start_in_query(k, carry):
        arriving_query(k).start()
        return carry

    lax.fori_loop(0, count, start_in, 0)
    lax.fori_loop(0, count, start_in_query, 0)

    barrier = pltpu.get_barrier_semaphore()
    peers = [at_y(s) for s in range(1, NY)] + [at_z(s) for s in range(1, NZ)] + [at_x(s) for s in range(1, NX)]
    peers = peers + [left_plane, right_plane]
    for peer in peers:
        pl.semaphore_signal(barrier, inc=1, device_id=(peer, core), device_id_type=MESH)
    pl.semaphore_signal(barrier, inc=1, device_id=(me, 1 - core), device_id_type=MESH)
    pl.semaphore_wait(barrier, len(peers) + 1)

    last = planes * NY - 1
    mine = cluster[me]
    on_left = cluster[jnp.maximum(me - NY, 0)]
    on_right = cluster[jnp.minimum(me + NY, last)]
    has_left = plane > 0
    has_right = plane < planes - 1
    want_left, want_right, linked = [], [], [None]
    for step in range(1, NY):
        target = at_y(step)
        theirs = cluster[target]
        want_left.append(has_left & (theirs == on_left))
        want_right.append(has_right & (theirs == on_right))
        near = theirs == mine
        near = near | (has_left & (cluster[jnp.maximum(target - NY, 0)] == mine))
        near = near | (has_right & (cluster[jnp.minimum(target + NY, last)] == mine))
        linked.append(near)

    def pick(step, here, from_left, from_right):
        return lax.select(
            want_left[step - 1], from_left, lax.select(want_right[step - 1], from_right, here)
        )

    def send(source, target, send_sem, recv_sem, place, where=None):
        return pltpu.make_async_remote_copy(
            src_ref=source, dst_ref=target, send_sem=send_sem, recv_sem=recv_sem,
            device_id=(place, core if where is None else where), device_id_type=MESH,
        )

    def along_z(k):
        return [
            send(own.at[k], beside.at[0, k], z_send.at[0, k], z_recv.at[0, k], right_plane),
            send(own.at[k], beside.at[1, k], z_send.at[1, k], z_recv.at[1, k], left_plane),
        ]

    def along_y(k):
        return [
            send(
                staged.at[s - 1, k], gathered.at[NY - s - 1, k],
                y_send.at[s - 1, k], y_recv.at[NY - s - 1, k], at_y(s),
            )
            for s in range(1, NY)
        ]

    def share(k):
        for copy in along_z(k):
            copy.start()

    def relay(k):
        for copy in along_z(k):
            copy.wait_recv()
        here, from_left, from_right = own[k], beside[0, k], beside[1, k]
        for s in range(1, NY):
            staged[s - 1, k] = pick(s, here, from_left, from_right)
        for copy in along_y(k):
            copy.start()

    def landed(k):
        for copy in along_y(k):
            copy.wait_recv()

    def block(k, slot):
        return own[k] if slot == 0 else gathered[slot - 1, k]

    def add_scores(k, first=False):
        mine_now = own[count + k]
        for slot in range(NY):
            columns = slice(slot * rows, (slot + 1) * rows)
            part = nt_dot(mine_now, block(k, slot))
            if first:
                score_own[:, columns] = part
            else:
                score_own[:, columns] += part

    def cast_passage(k):
        arriving(k).wait()
        own[k] = fresh[k].astype(jnp.bfloat16)

    for k in range(3):
        cast_passage(k)
        share(k)

    def cast_rest(k, carry):
        cast_passage(k)
        return carry

    def cast_queries(k, carry):
        arriving_query(k).wait()
        own[count + k] = fresh[count + k].astype(jnp.bfloat16)
        return carry

    lax.fori_loop(3, count, cast_rest, 0)
    lax.fori_loop(0, count, cast_queries, 0)

    for part in range(rows // 128):
        here = slice(part * 128, (part + 1) * 128)
        as_row = positive[part : part + 1, :].astype(jnp.float32)
        pos_cols[here, :] = jnp.broadcast_to(as_row, (128, 128)).T
        weight_cols[here, :] = jnp.broadcast_to(weight[part : part + 1, :], (128, 128)).T

    relay(0)
    share(3)
    relay(1)
    share(4)
    landed(0)
    add_scores(0, first=True)

    def passage_step(k, carry):
        relay(k)
        share(k + 3)
        landed(k - 1)
        add_scores(k - 1)
        return carry

    lax.fori_loop(2, count, passage_step, 0)
    relay(count)
    share(count + 3)
    landed(count - 1)
    add_scores(count - 1)
    swap = send(score_own, score_other, s_send, s_recv, me, 1 - core)
    swap.start()
    relay(count + 1)
    share(count + 4)
    swap.wait_recv()

    scale = 3.0 / math.sqrt(2 * width)

    def soft_rows(group, total):
        here = pl.ds(pl.multiple_of(group * GROUP, GROUP), GROUP)
        tiles = []
        for slot in range(NY):
            columns = slice(slot * rows, (slot + 1) * rows)
            tile = (score_own[here, columns] + score_other[here, columns]) * scale
            if slot > 0:
                tile = lax.select(linked[slot], tile, jnp.full_like(tile, -1e30))
            tiles.append(tile)
        top = functools.reduce(jnp.maximum, [jnp.max(t, axis=1, keepdims=True) for t in tiles])
        expo = [jnp.exp(t - top) for t in tiles]
        row_total = functools.reduce(jnp.add, [jnp.sum(e, axis=1, keepdims=True) for e in expo])
        wanted = pos_cols[here, 0:1]
        heavy = weight_cols[here, 0:1]
        columns = lax.broadcasted_iota(jnp.int32, (GROUP, rows), 1).astype(jnp.float32)
        hit = columns == wanted
        picked = jnp.sum(jnp.where(hit, tiles[0], 0.0), axis=1, keepdims=True)
        ratio = heavy / row_total
        for slot in range(NY):
            value = expo[slot] * ratio
            if slot == 0:
                value = value - jnp.where(hit, heavy, 0.0)
            coeff[slot, here, :] = value.astype(jnp.bfloat16)
        return total + heavy * (top + jnp.log(row_total) - picked)

    total = lax.fori_loop(0, rows // GROUP, soft_rows, jnp.zeros((GROUP, 1), jnp.float32))
    loss_tile[...] = jnp.broadcast_to(jnp.sum(total, axis=0, keepdims=True), loss_tile.shape)

    my_half = pl.ds(pl.multiple_of(core * half, half), half)
    for s in range(1, NY):
        coeff_out[s - 1] = coeff[s, my_half, :]
    coeff_z = [
        send(coeff_out, coeff_beside.at[0], cz_send.at[0], cz_recv.at[0], right_plane),
        send(coeff_out, coeff_beside.at[1], cz_send.at[1], cz_recv.at[1], left_plane),
    ]
    for copy in coeff_z:
        copy.start()

    def spread(buffer, send_sem, recv_sem, mine_at, size, place):
        return [
            send(loss_tile, buffer.at[mine_at], send_sem.at[s - 1], recv_sem.at[mine_at], place(s))
            for s in range(1, size)
        ]

    def collect(buffer, recv_sem, mine_at, size):
        buffer[mine_at] = loss_tile[...]
        for s in range(1, size):
            source = (mine_at + s) % size
            send(loss_tile, buffer.at[source], recv_sem.at[source], recv_sem.at[source], me, 1 - core).wait_recv()
        value = buffer[0]
        for s in range(1, size):
            value = value + buffer[s]
        return value

    loss_along_y = spread(loss_y, ly_send, ly_recv, y, NY, at_y)
    for copy in loss_along_y:
        copy.start()

    landed(count)
    relay(count + 2)
    share(count + 5)

    def query_grad_step(k, carry):
        value = nn_dot(coeff[0], own[k])
        for slot in range(1, NY):
            value = value + nn_dot(coeff[slot], gathered[slot - 1, k])
        query_grad[k] = value
        start = pl.multiple_of(k * CHUNK, CHUNK)
        pltpu.make_async_copy(query_grad.at[k], query_grad_hbm.at[:, pl.ds(start, CHUNK)], qg_sem.at[k]).start()
        return carry

    lax.fori_loop(0, count, query_grad_step, 0)

    for copy in coeff_z:
        copy.wait_recv()
    for s in range(1, NY):
        coeff_staged[s - 1] = pick(s, coeff_out[s - 1], coeff_beside[0, s - 1], coeff_beside[1, s - 1])
    coeff_y = [
        send(
            coeff_staged.at[s - 1], coeff_got.at[NY - s - 1], cy_send.at[s - 1], cy_recv.at[NY - s - 1], at_y(s)
        )
        for s in range(1, NY)
    ]
    for copy in coeff_y:
        copy.start()

    landed(count + 1)
    relay(count + 3)
    share(count + 6)
    value = collect(loss_y, ly_recv, y, NY)
    for copy in loss_along_y:
        copy.wait_send()
    loss_tile[...] = value
    loss_along_z = spread(loss_z, lz_send, lz_recv, z, NZ, at_z)
    for copy in loss_along_z:
        copy.start()

    landed(count + 2)
    relay(count + 4)
    share(count + 7)
    for copy in coeff_y:
        copy.wait_recv()
    forward = send(coeff_got, coeff_fwd, cf_send, cf_recv, me, 1 - core)
    forward.start()
    value = collect(loss_z, lz_recv, z, NZ)
    for copy in loss_along_z:
        copy.wait_send()
    loss_tile[...] = value
    loss_along_x = spread(loss_x, lx_send, lx_recv, x, NX, at_x)
    for copy in loss_along_x:
        copy.start()

    landed(count + 3)
    relay(count + 5)
    forward.wait_recv()

    coeff_t[0] = coeff[0].astype(jnp.float32).T.astype(jnp.bfloat16)
    first_half = core == 0
    for slot in range(1, NY):
        got, fwd = coeff_got[slot - 1], coeff_fwd[slot - 1]
        tile = jnp.concatenate([lax.select(first_half, got, fwd), lax.select(first_half, fwd, got)], axis=0)
        tile = tile.astype(jnp.float32).T
        tile = lax.select(linked[slot], tile, jnp.zeros_like(tile))
        coeff_t[slot] = tile.astype(jnp.bfloat16)

    landed(count + 4)
    relay(count + 6)
    value = collect(loss_x, lx_recv, x, NX)
    for copy in loss_along_x:
        copy.wait_send()
    loss_ref[...] = value * (1.0 / (rows * planes * NY))

    def passage_grad_out(k):
        start = pl.multiple_of(k * CHUNK, CHUNK)
        return pltpu.make_async_copy(
            passage_grad.at[k], passage_grad_hbm.at[:, pl.ds(start, CHUNK)], pg_sem.at[k]
        )

    def passage_grad_step(k, carry):
        value = nn_dot(coeff_t[0], own[count + k])
        for slot in range(1, NY):
            value = value + nn_dot(coeff_t[slot], gathered[slot - 1, count + k])
        passage_grad[k] = value
        passage_grad_out(k).start()
        return carry

    landed(count + 5)
    relay(count + 7)
    lax.fori_loop(0, 6, passage_grad_step, 0)
    landed(count + 6)
    passage_grad_step(6, 0)
    landed(count + 7)
    passage_grad_step(7, 0)

    def finish_sends(k, carry):
        for copy in along_z(k):
            copy.wait_send()
        for copy in along_y(k):
            copy.wait_send()
        return carry

    lax.fori_loop(0, 2 * count, finish_sends, 0)
    for copy in coeff_z + coeff_y + [swap, forward]:
        copy.wait_send()

    def finish_out(k, carry):
        start = pl.multiple_of(k * CHUNK, CHUNK)
        pltpu.make_async_copy(query_grad.at[k], query_grad_hbm.at[:, pl.ds(start, CHUNK)], qg_sem.at[k]).wait()
        passage_grad_out(k).wait()
        return carry

    lax.fori_loop(0, count, finish_out, 0)


def shards(queries, passages, cluster_of_block, positive_row, query_weight):
    rows, width = queries.shape
    count = width // CHUNK
    dma = pltpu.SemaphoreType.DMA
    vmem = pltpu.VMEM
    low, full = jnp.bfloat16, jnp.float32
    tile = (8, 128)
    scratch = [
        vmem((2 * count, rows, CHUNK), full),
        vmem((2 * count, rows, CHUNK), low),
        vmem((2, 2 * count, rows, CHUNK), low),
        vmem((NY - 1, 2 * count, rows, CHUNK), low),
        vmem((NY - 1, 2 * count, rows, CHUNK), low),
        vmem((rows, NY * rows), full),
        vmem((rows, NY * rows), full),
        vmem((NY, rows, rows), low),
        vmem((NY - 1, rows // 2, rows), low),
        vmem((2, NY - 1, rows // 2, rows), low),
        vmem((NY - 1, rows // 2, rows), low),
        vmem((NY - 1, rows // 2, rows), low),
        vmem((NY - 1, rows // 2, rows), low),
        vmem((NY, rows, rows), low),
        vmem((rows, 128), full),
        vmem((rows, 128), full),
        vmem((count, rows, CHUNK), full),
        vmem((count, rows, CHUNK), full),
        vmem(tile, full),
        vmem((NY,) + tile, full),
        vmem((NZ,) + tile, full),
        vmem((NX,) + tile, full),
        dma((2 * count,)),
        dma((2, 2 * count)),
        dma((2, 2 * count)),
        dma((NY - 1, 2 * count)),
        dma((NY - 1, 2 * count)),
        dma, dma,
        dma((2,)), dma((2,)),
        dma((NY - 1,)), dma((NY - 1,)),
        dma, dma,
        dma((NY,)), dma((NY,)),
        dma((NZ,)), dma((NZ,)),
        dma((NX,)), dma((NX,)),
        dma((count,)), dma((count,)),
    ]
    anywhere = pl.BlockSpec(memory_space=pl.ANY)
    in_vmem = pl.BlockSpec(memory_space=pltpu.VMEM)
    loss, query_grad, passage_grad = pl.pallas_call(
        kernel,
        out_shape=[
            jax.ShapeDtypeStruct(tile, full),
            jax.ShapeDtypeStruct((rows, width), full),
            jax.ShapeDtypeStruct((rows, width), full),
        ],
        in_specs=[anywhere, anywhere, pl.BlockSpec(memory_space=pltpu.SMEM), in_vmem, in_vmem],
        out_specs=[in_vmem, anywhere, anywhere],
        scratch_shapes=scratch,
        compiler_params=pltpu.CompilerParams(
            collective_id=0, has_side_effects=True, vmem_limit_bytes=56 * 2**20
        ),
        cost_estimate=pl.CostEstimate(
            flops=6 * NY * rows * rows * width, bytes_accessed=16 * rows * width, transcendentals=NY * rows * rows
        ),
    )(
        queries, passages, cluster_of_block,
        positive_row.reshape(rows // 128, 128), query_weight.reshape(rows // 128, 128),
    )
    return loss[0, 0], query_grad, passage_grad


def solution(mesh):
    in_specs = (P("dp", "mp"), P("dp", "mp"), P(), P("dp"), P("dp"))
    out_specs = (P(), P("dp", "mp"), P("dp", "mp"))
    return jax.shard_map(shards, mesh=mesh, in_specs=in_specs, out_specs=out_specs, check_vma=False)
```

```python
import functools
import math

import jax
import jax.numpy as jnp
from jax import lax
from jax.experimental import pallas as pl
from jax.experimental.pallas import tpu as pltpu
from jax.sharding import PartitionSpec as P

MESH = pl.DeviceIdType.MESH
NY, NZ, NX = 4, 8, 4
CHUNK = 256
GROUP = 32


def nt_dot(left, right):
    return lax.dot_general(left, right, (((1,), (1,)), ((), ())), preferred_element_type=jnp.float32)


def nn_dot(left, right):
    return jnp.dot(left, right, preferred_element_type=jnp.float32)


def kernel(
    query_hbm, passage_hbm, cluster, positive, weight,
    loss_ref, query_grad, passage_grad,
    fresh, own, beside, staged, gathered, raw, raw_beside,
    score_own, score_other, coeff, coeff_out, coeff_beside, coeff_staged, coeff_got, coeff_fwd, coeff_t,
    pos_cols, weight_cols, loss_tile, loss_y, loss_z, loss_x,
    in_sem, z_send, z_recv, y_send, y_recv, s_send, s_recv,
    cz_send, cz_recv, cy_send, cy_recv, cf_send, cf_recv,
    ly_send, ly_recv, lz_send, lz_recv, lx_send, lx_recv, raw_send, raw_recv,
):
    rows, width = query_hbm.shape
    count = width // CHUNK
    half = rows // 2
    planes = NX * NZ
    me = lax.axis_index("dp")
    core = lax.axis_index("mp")
    y = me % NY
    plane = me // NY
    z = plane % NZ
    x = plane // NZ

    def at_y(step):
        return plane * NY + (y + step) % NY

    def at_z(step):
        return (x * NZ + (z + step) % NZ) * NY + y

    def at_x(step):
        return (((x + step) % NX) * NZ + z) * NY + y

    left_plane = ((plane + planes - 1) % planes) * NY + y
    right_plane = ((plane + 1) % planes) * NY + y

    def arriving(k):
        start = pl.multiple_of(k * CHUNK, CHUNK)
        return pltpu.make_async_copy(passage_hbm.at[:, pl.ds(start, CHUNK)], fresh.at[k], in_sem.at[k])

    def arriving_query(k):
        start = pl.multiple_of(k * CHUNK, CHUNK)
        return pltpu.make_async_copy(
            query_hbm.at[:, pl.ds(start, CHUNK)], fresh.at[count + k], in_sem.at[count + k]
        )

    def start_in(k, carry):
        arriving(k).start()
        return carry

    def start_in_query(k, carry):
        arriving_query(k).start()
        return carry

    lax.fori_loop(0, count, start_in, 0)
    lax.fori_loop(0, count, start_in_query, 0)

    barrier = pltpu.get_barrier_semaphore()
    peers = [at_y(s) for s in range(1, NY)] + [at_z(s) for s in range(1, NZ)] + [at_x(s) for s in range(1, NX)]
    peers = peers + [left_plane, right_plane]
    for peer in peers:
        pl.semaphore_signal(barrier, inc=1, device_id=(peer, core), device_id_type=MESH)
    pl.semaphore_signal(barrier, inc=1, device_id=(me, 1 - core), device_id_type=MESH)
    pl.semaphore_wait(barrier, len(peers) + 1)

    last = planes * NY - 1
    mine = cluster[me]
    on_left = cluster[jnp.maximum(me - NY, 0)]
    on_right = cluster[jnp.minimum(me + NY, last)]
    has_left = plane > 0
    has_right = plane < planes - 1
    want_left, want_right, linked = [], [], [None]
    got_left, got_right = [None], [None]
    for step in range(1, NY):
        target = at_y(step)
        theirs = cluster[target]
        want_left.append(has_left & (theirs == on_left))
        want_right.append(has_right & (theirs == on_right))
        from_here = theirs == mine
        from_left = has_left & (cluster[jnp.maximum(target - NY, 0)] == mine)
        from_right = has_right & (cluster[jnp.minimum(target + NY, last)] == mine)
        linked.append(from_here | from_left | from_right)
        got_left.append(from_left)
        got_right.append(from_right)

    def pick(step, here, from_left, from_right):
        return lax.select(
            want_left[step - 1], from_left, lax.select(want_right[step - 1], from_right, here)
        )

    def send(source, target, send_sem, recv_sem, place, where=None):
        return pltpu.make_async_remote_copy(
            src_ref=source, dst_ref=target, send_sem=send_sem, recv_sem=recv_sem,
            device_id=(place, core if where is None else where), device_id_type=MESH,
        )

    def along_z(k):
        return [
            send(own.at[k], beside.at[0, k], z_send.at[0, k], z_recv.at[0, k], right_plane),
            send(own.at[k], beside.at[1, k], z_send.at[1, k], z_recv.at[1, k], left_plane),
        ]

    def along_y(k):
        return [
            send(
                staged.at[s - 1, k], gathered.at[NY - s - 1, k],
                y_send.at[s - 1, k], y_recv.at[NY - s - 1, k], at_y(s),
            )
            for s in range(1, NY)
        ]

    def share(k):
        for copy in along_z(k):
            copy.start()

    def relay(k):
        for copy in along_z(k):
            copy.wait_recv()
        here, from_left, from_right = own[k], beside[0, k], beside[1, k]
        for s in range(1, NY):
            staged[s - 1, k] = pick(s, here, from_left, from_right)
        for copy in along_y(k):
            copy.start()

    def landed(k):
        for copy in along_y(k):
            copy.wait_recv()

    def block(k, slot):
        return own[k] if slot == 0 else gathered[slot - 1, k]

    def add_scores(k, first=False):
        mine_now = own[count + k]
        for slot in range(NY):
            columns = slice(slot * rows, (slot + 1) * rows)
            part = nt_dot(mine_now, block(k, slot))
            if first:
                score_own[:, columns] = part
            else:
                score_own[:, columns] += part

    def cast_passage(k):
        arriving(k).wait()
        own[k] = fresh[k].astype(jnp.bfloat16)

    def first_along_y():
        return [
            send(own.at[0], raw.at[NY - s - 1], y_send.at[s - 1, 0], y_recv.at[NY - s - 1, 0], at_y(s))
            for s in range(1, NY)
        ]

    def first_along_z():
        return [
            send(raw, raw_beside.at[0], raw_send.at[0], raw_recv.at[0], right_plane),
            send(raw, raw_beside.at[1], raw_send.at[1], raw_recv.at[1], left_plane),
        ]

    cast_passage(0)
    for copy in first_along_y():
        copy.start()
    for k in range(1, 4):
        cast_passage(k)
        share(k)

    def cast_rest(k, carry):
        cast_passage(k)
        return carry

    def cast_queries(k, carry):
        arriving_query(k).wait()
        own[count + k] = fresh[count + k].astype(jnp.bfloat16)
        return carry

    lax.fori_loop(4, count, cast_rest, 0)
    lax.fori_loop(0, count, cast_queries, 0)

    for part in range(rows // 128):
        here = slice(part * 128, (part + 1) * 128)
        as_row = positive[part : part + 1, :].astype(jnp.float32)
        pos_cols[here, :] = jnp.broadcast_to(as_row, (128, 128)).T
        weight_cols[here, :] = jnp.broadcast_to(weight[part : part + 1, :], (128, 128)).T

    relay(1)
    share(4)
    for copy in first_along_y():
        copy.wait_recv()
    relay(2)
    share(5)
    landed(1)
    add_scores(1, first=True)

    def passage_step(k, carry):
        relay(k)
        share(k + 3)
        landed(k - 1)
        add_scores(k - 1)
        return carry

    passage_step(3, 0)
    for copy in first_along_z():
        copy.start()
    lax.fori_loop(4, count, passage_step, 0)
    for copy in first_along_z():
        copy.wait_recv()
    for slot in range(1, NY):
        gathered[slot - 1, 0] = lax.select(
            got_left[slot], raw_beside[0, slot - 1],
            lax.select(got_right[slot], raw_beside[1, slot - 1], raw[slot - 1]),
        )
    add_scores(0)
    relay(count)
    share(count + 3)
    landed(count - 1)
    add_scores(count - 1)
    swap = send(score_own, score_other, s_send, s_recv, me, 1 - core)
    swap.start()
    relay(count + 1)
    share(count + 4)
    swap.wait_recv()

    scale = 3.0 / math.sqrt(2 * width)

    def soft_rows(group, total):
        here = pl.ds(pl.multiple_of(group * GROUP, GROUP), GROUP)
        tiles = []
        for slot in range(NY):
            columns = slice(slot * rows, (slot + 1) * rows)
            tile = (score_own[here, columns] + score_other[here, columns]) * scale
            if slot > 0:
                tile = lax.select(linked[slot], tile, jnp.full_like(tile, -1e30))
            tiles.append(tile)
        top = functools.reduce(jnp.maximum, [jnp.max(t, axis=1, keepdims=True) for t in tiles])
        expo = [jnp.exp(t - top) for t in tiles]
        row_total = functools.reduce(jnp.add, [jnp.sum(e, axis=1, keepdims=True) for e in expo])
        wanted = pos_cols[here, 0:1]
        heavy = weight_cols[here, 0:1]
        columns = lax.broadcasted_iota(jnp.int32, (GROUP, rows), 1).astype(jnp.float32)
        hit = columns == wanted
        picked = jnp.sum(jnp.where(hit, tiles[0], 0.0), axis=1, keepdims=True)
        ratio = heavy / row_total
        for slot in range(NY):
            value = expo[slot] * ratio
            if slot == 0:
                value = value - jnp.where(hit, heavy, 0.0)
            coeff[slot, here, :] = value.astype(jnp.bfloat16)
        return total + heavy * (top + jnp.log(row_total) - picked)

    total = lax.fori_loop(0, rows // GROUP, soft_rows, jnp.zeros((GROUP, 1), jnp.float32))
    loss_tile[...] = jnp.broadcast_to(jnp.sum(total, axis=0, keepdims=True), loss_tile.shape)

    my_half = pl.ds(pl.multiple_of(core * half, half), half)
    for s in range(1, NY):
        coeff_out[s - 1] = coeff[s, my_half, :]
    coeff_z = [
        send(coeff_out, coeff_beside.at[0], cz_send.at[0], cz_recv.at[0], right_plane),
        send(coeff_out, coeff_beside.at[1], cz_send.at[1], cz_recv.at[1], left_plane),
    ]
    for copy in coeff_z:
        copy.start()

    def spread(buffer, send_sem, recv_sem, mine_at, size, place):
        return [
            send(loss_tile, buffer.at[mine_at], send_sem.at[s - 1], recv_sem.at[mine_at], place(s))
            for s in range(1, size)
        ]

    def collect(buffer, recv_sem, mine_at, size):
        buffer[mine_at] = loss_tile[...]
        for s in range(1, size):
            source = (mine_at + s) % size
            send(loss_tile, buffer.at[source], recv_sem.at[source], recv_sem.at[source], me, 1 - core).wait_recv()
        value = buffer[0]
        for s in range(1, size):
            value = value + buffer[s]
        return value

    loss_along_y = spread(loss_y, ly_send, ly_recv, y, NY, at_y)
    for copy in loss_along_y:
        copy.start()

    landed(count)
    relay(count + 2)
    share(count + 5)

    def query_grad_step(k, carry):
        value = nn_dot(coeff[0], own[k])
        for slot in range(1, NY):
            value = value + nn_dot(coeff[slot], gathered[slot - 1, k])
        query_grad[:, pl.ds(pl.multiple_of(k * CHUNK, CHUNK), CHUNK)] = value
        return carry

    lax.fori_loop(0, count, query_grad_step, 0)

    for copy in coeff_z:
        copy.wait_recv()
    for s in range(1, NY):
        coeff_staged[s - 1] = pick(s, coeff_out[s - 1], coeff_beside[0, s - 1], coeff_beside[1, s - 1])
    coeff_y = [
        send(
            coeff_staged.at[s - 1], coeff_got.at[NY - s - 1], cy_send.at[s - 1], cy_recv.at[NY - s - 1], at_y(s)
        )
        for s in range(1, NY)
    ]
    for copy in coeff_y:
        copy.start()

    landed(count + 1)
    relay(count + 3)
    share(count + 6)
    value = collect(loss_y, ly_recv, y, NY)
    for copy in loss_along_y:
        copy.wait_send()
    loss_tile[...] = value
    loss_along_z = spread(loss_z, lz_send, lz_recv, z, NZ, at_z)
    for copy in loss_along_z:
        copy.start()

    landed(count + 2)
    relay(count + 4)
    share(count + 7)
    for copy in coeff_y:
        copy.wait_recv()
    forward = send(coeff_got, coeff_fwd, cf_send, cf_recv, me, 1 - core)
    forward.start()
    value = collect(loss_z, lz_recv, z, NZ)
    for copy in loss_along_z:
        copy.wait_send()
    loss_tile[...] = value
    loss_along_x = spread(loss_x, lx_send, lx_recv, x, NX, at_x)
    for copy in loss_along_x:
        copy.start()

    landed(count + 3)
    relay(count + 5)
    forward.wait_recv()

    coeff_t[0] = coeff[0].astype(jnp.float32).T.astype(jnp.bfloat16)
    first_half = core == 0
    for slot in range(1, NY):
        got, fwd = coeff_got[slot - 1], coeff_fwd[slot - 1]
        tile = jnp.concatenate([lax.select(first_half, got, fwd), lax.select(first_half, fwd, got)], axis=0)
        tile = tile.astype(jnp.float32).T
        tile = lax.select(linked[slot], tile, jnp.zeros_like(tile))
        coeff_t[slot] = tile.astype(jnp.bfloat16)

    landed(count + 4)
    relay(count + 6)
    value = collect(loss_x, lx_recv, x, NX)
    for copy in loss_along_x:
        copy.wait_send()
    loss_ref[...] = value * (1.0 / (rows * planes * NY))

    def passage_grad_step(k, carry):
        value = nn_dot(coeff_t[0], own[count + k])
        for slot in range(1, NY):
            value = value + nn_dot(coeff_t[slot], gathered[slot - 1, count + k])
        passage_grad[:, pl.ds(pl.multiple_of(k * CHUNK, CHUNK), CHUNK)] = value
        return carry

    landed(count + 5)
    relay(count + 7)
    lax.fori_loop(0, 6, passage_grad_step, 0)
    landed(count + 6)
    passage_grad_step(6, 0)
    landed(count + 7)
    passage_grad_step(7, 0)

    def finish_sends(k, carry):
        for copy in along_z(k):
            copy.wait_send()
        for copy in along_y(k):
            copy.wait_send()
        return carry

    lax.fori_loop(1, 2 * count, finish_sends, 0)
    for copy in first_along_y() + first_along_z() + coeff_z + coeff_y + [swap, forward]:
        copy.wait_send()


def shards(queries, passages, cluster_of_block, positive_row, query_weight):
    rows, width = queries.shape
    count = width // CHUNK
    dma = pltpu.SemaphoreType.DMA
    vmem = pltpu.VMEM
    low, full = jnp.bfloat16, jnp.float32
    tile = (8, 128)
    scratch = [
        vmem((2 * count, rows, CHUNK), full),
        vmem((2 * count, rows, CHUNK), low),
        vmem((2, 2 * count, rows, CHUNK), low),
        vmem((NY - 1, 2 * count, rows, CHUNK), low),
        vmem((NY - 1, 2 * count, rows, CHUNK), low),
        vmem((NY - 1, rows, CHUNK), low),
        vmem((2, NY - 1, rows, CHUNK), low),
        vmem((rows, NY * rows), full),
        vmem((rows, NY * rows), full),
        vmem((NY, rows, rows), low),
        vmem((NY - 1, rows // 2, rows), low),
        vmem((2, NY - 1, rows // 2, rows), low),
        vmem((NY - 1, rows // 2, rows), low),
        vmem((NY - 1, rows // 2, rows), low),
        vmem((NY - 1, rows // 2, rows), low),
        vmem((NY, rows, rows), low),
        vmem((rows, 128), full),
        vmem((rows, 128), full),
        vmem(tile, full),
        vmem((NY,) + tile, full),
        vmem((NZ,) + tile, full),
        vmem((NX,) + tile, full),
        dma((2 * count,)),
        dma((2, 2 * count)),
        dma((2, 2 * count)),
        dma((NY - 1, 2 * count)),
        dma((NY - 1, 2 * count)),
        dma, dma,
        dma((2,)), dma((2,)),
        dma((NY - 1,)), dma((NY - 1,)),
        dma, dma,
        dma((NY,)), dma((NY,)),
        dma((NZ,)), dma((NZ,)),
        dma((NX,)), dma((NX,)),
        dma((2,)), dma((2,)),
    ]
    anywhere = pl.BlockSpec(memory_space=pl.ANY)
    in_vmem = pl.BlockSpec(memory_space=pltpu.VMEM)
    loss, query_grad, passage_grad = pl.pallas_call(
        kernel,
        out_shape=[
            jax.ShapeDtypeStruct(tile, full),
            vmem((rows, width), full),
            vmem((rows, width), full),
        ],
        in_specs=[anywhere, anywhere, pl.BlockSpec(memory_space=pltpu.SMEM), in_vmem, in_vmem],
        out_specs=[in_vmem, in_vmem, in_vmem],
        scratch_shapes=scratch,
        compiler_params=pltpu.CompilerParams(
            collective_id=0, has_side_effects=True, vmem_limit_bytes=48 * 2**20
        ),
        cost_estimate=pl.CostEstimate(
            flops=6 * NY * rows * rows * width, bytes_accessed=16 * rows * width, transcendentals=NY * rows * rows
        ),
    )(
        queries, passages, cluster_of_block,
        positive_row.reshape(rows // 128, 128), query_weight.reshape(rows // 128, 128),
    )
    return loss[0, 0], query_grad, passage_grad


def solution(mesh):
    in_specs = (P("dp", "mp"), P("dp", "mp"), P(), P("dp"), P("dp"))
    out_specs = (P(), P("dp", "mp"), P("dp", "mp"))
    return jax.shard_map(shards, mesh=mesh, in_specs=in_specs, out_specs=out_specs, check_vma=False)
```

```python
import functools
import math

import jax
import jax.numpy as jnp
from jax import lax
from jax.experimental import pallas as pl
from jax.experimental.pallas import tpu as pltpu
from jax.sharding import PartitionSpec as P

MESH = pl.DeviceIdType.MESH
NY, NZ, NX = 4, 8, 4
CHUNK = 256
GROUP = 32


def nt_dot(left, right):
    return lax.dot_general(left, right, (((1,), (1,)), ((), ())), preferred_element_type=jnp.float32)


def nn_dot(left, right):
    return jnp.dot(left, right, preferred_element_type=jnp.float32)


def kernel(
    query_hbm, passage_hbm, cluster_hbm, positive_hbm, weight_hbm,
    loss_ref, query_grad, passage_grad,
    cluster, positive, weight, fresh, own, beside, staged, gathered, raw, raw_beside,
    score_own, score_other, coeff, coeff_out, coeff_beside, coeff_staged, coeff_got, coeff_fwd, coeff_t,
    pos_cols, weight_cols, loss_tile, loss_y, loss_z, loss_x,
    in_sem, z_send, z_recv, y_send, y_recv, s_send, s_recv,
    cz_send, cz_recv, cy_send, cy_recv, cf_send, cf_recv,
    ly_send, ly_recv, lz_send, lz_recv, lx_send, lx_recv, raw_send, raw_recv, small_sem,
):
    rows, width = query_hbm.shape
    count = width // CHUNK
    half = rows // 2
    planes = NX * NZ
    me = lax.axis_index("dp")
    core = lax.axis_index("mp")
    y = me % NY
    plane = me // NY
    z = plane % NZ
    x = plane // NZ

    def at_y(step):
        return plane * NY + (y + step) % NY

    def at_z(step):
        return (x * NZ + (z + step) % NZ) * NY + y

    def at_x(step):
        return (((x + step) % NX) * NZ + z) * NY + y

    left_plane = ((plane + planes - 1) % planes) * NY + y
    right_plane = ((plane + 1) % planes) * NY + y

    def arriving(k):
        start = pl.multiple_of(k * CHUNK, CHUNK)
        return pltpu.make_async_copy(passage_hbm.at[:, pl.ds(start, CHUNK)], fresh.at[k], in_sem.at[k])

    def arriving_query(k):
        start = pl.multiple_of(k * CHUNK, CHUNK)
        return pltpu.make_async_copy(
            query_hbm.at[:, pl.ds(start, CHUNK)], fresh.at[count + k], in_sem.at[count + k]
        )

    def start_in(k, carry):
        arriving(k).start()
        return carry

    def start_in_query(k, carry):
        arriving_query(k).start()
        return carry

    small = [
        pltpu.make_async_copy(source, target, small_sem.at[i])
        for i, (source, target) in enumerate(
            [(cluster_hbm, cluster), (positive_hbm, positive), (weight_hbm, weight)]
        )
    ]
    arriving(0).start()
    for copy in small:
        copy.start()
    lax.fori_loop(1, count, start_in, 0)
    lax.fori_loop(0, count, start_in_query, 0)

    barrier = pltpu.get_barrier_semaphore()
    peers = [at_y(s) for s in range(1, NY)] + [at_z(s) for s in range(1, NZ)] + [at_x(s) for s in range(1, NX)]
    peers = peers + [left_plane, right_plane]
    for peer in peers:
        pl.semaphore_signal(barrier, inc=1, device_id=(peer, core), device_id_type=MESH)
    pl.semaphore_signal(barrier, inc=1, device_id=(me, 1 - core), device_id_type=MESH)
    pl.semaphore_wait(barrier, len(peers) + 1)

    for copy in small:
        copy.wait()

    last = planes * NY - 1
    mine = cluster[me]
    on_left = cluster[jnp.maximum(me - NY, 0)]
    on_right = cluster[jnp.minimum(me + NY, last)]
    has_left = plane > 0
    has_right = plane < planes - 1
    want_left, want_right, linked = [], [], [None]
    got_left, got_right = [None], [None]
    for step in range(1, NY):
        target = at_y(step)
        theirs = cluster[target]
        want_left.append(has_left & (theirs == on_left))
        want_right.append(has_right & (theirs == on_right))
        from_here = theirs == mine
        from_left = has_left & (cluster[jnp.maximum(target - NY, 0)] == mine)
        from_right = has_right & (cluster[jnp.minimum(target + NY, last)] == mine)
        linked.append(from_here | from_left | from_right)
        got_left.append(from_left)
        got_right.append(from_right)

    def pick(step, here, from_left, from_right):
        return lax.select(
            want_left[step - 1], from_left, lax.select(want_right[step - 1], from_right, here)
        )

    def send(source, target, send_sem, recv_sem, place, where=None):
        return pltpu.make_async_remote_copy(
            src_ref=source, dst_ref=target, send_sem=send_sem, recv_sem=recv_sem,
            device_id=(place, core if where is None else where), device_id_type=MESH,
        )

    def along_z(k):
        return [
            send(own.at[k], beside.at[0, k], z_send.at[0, k], z_recv.at[0, k], right_plane),
            send(own.at[k], beside.at[1, k], z_send.at[1, k], z_recv.at[1, k], left_plane),
        ]

    def along_y(k):
        return [
            send(
                staged.at[s - 1, k], gathered.at[NY - s - 1, k],
                y_send.at[s - 1, k], y_recv.at[NY - s - 1, k], at_y(s),
            )
            for s in range(1, NY)
        ]

    def share(k):
        for copy in along_z(k):
            copy.start()

    def relay(k):
        for copy in along_z(k):
            copy.wait_recv()
        here, from_left, from_right = own[k], beside[0, k], beside[1, k]
        for s in range(1, NY):
            staged[s - 1, k] = pick(s, here, from_left, from_right)
        for copy in along_y(k):
            copy.start()

    def landed(k):
        for copy in along_y(k):
            copy.wait_recv()

    def block(k, slot):
        return own[k] if slot == 0 else gathered[slot - 1, k]

    def add_scores(k, first=False):
        mine_now = own[count + k]
        for slot in range(NY):
            columns = slice(slot * rows, (slot + 1) * rows)
            part = nt_dot(mine_now, block(k, slot))
            if first:
                score_own[:, columns] = part
            else:
                score_own[:, columns] += part

    def cast_passage(k):
        arriving(k).wait()
        own[k] = fresh[k].astype(jnp.bfloat16)

    def first_along_y():
        return [
            send(own.at[0], raw.at[NY - s - 1], y_send.at[s - 1, 0], y_recv.at[NY - s - 1, 0], at_y(s))
            for s in range(1, NY)
        ]

    def first_along_z():
        return [
            send(raw, raw_beside.at[0], raw_send.at[0], raw_recv.at[0], right_plane),
            send(raw, raw_beside.at[1], raw_send.at[1], raw_recv.at[1], left_plane),
        ]

    cast_passage(0)
    for copy in first_along_y():
        copy.start()
    for k in range(1, 4):
        cast_passage(k)
        share(k)

    def cast_rest(k, carry):
        cast_passage(k)
        return carry

    def cast_queries(k, carry):
        arriving_query(k).wait()
        own[count + k] = fresh[count + k].astype(jnp.bfloat16)
        return carry

    lax.fori_loop(4, count, cast_rest, 0)
    lax.fori_loop(0, count, cast_queries, 0)

    for part in range(rows // 128):
        here = slice(part * 128, (part + 1) * 128)
        as_row = positive[part : part + 1, :].astype(jnp.float32)
        pos_cols[here, :] = jnp.broadcast_to(as_row, (128, 128)).T
        weight_cols[here, :] = jnp.broadcast_to(weight[part : part + 1, :], (128, 128)).T

    relay(1)
    share(4)
    for copy in first_along_y():
        copy.wait_recv()
    relay(2)
    share(5)
    landed(1)
    add_scores(1, first=True)

    def passage_step(k, carry):
        relay(k)
        share(k + 3)
        landed(k - 1)
        add_scores(k - 1)
        return carry

    passage_step(3, 0)
    for copy in first_along_z():
        copy.start()
    lax.fori_loop(4, count, passage_step, 0)
    for copy in first_along_z():
        copy.wait_recv()
    for slot in range(1, NY):
        gathered[slot - 1, 0] = lax.select(
            got_left[slot], raw_beside[0, slot - 1],
            lax.select(got_right[slot], raw_beside[1, slot - 1], raw[slot - 1]),
        )
    add_scores(0)
    relay(count)
    share(count + 3)
    landed(count - 1)
    add_scores(count - 1)
    swap = send(score_own, score_other, s_send, s_recv, me, 1 - core)
    swap.start()
    relay(count + 1)
    share(count + 4)
    swap.wait_recv()

    scale = 3.0 / math.sqrt(2 * width)

    def soft_rows(group, total):
        here = pl.ds(pl.multiple_of(group * GROUP, GROUP), GROUP)
        tiles = []
        for slot in range(NY):
            columns = slice(slot * rows, (slot + 1) * rows)
            tile = (score_own[here, columns] + score_other[here, columns]) * scale
            if slot > 0:
                tile = lax.select(linked[slot], tile, jnp.full_like(tile, -1e30))
            tiles.append(tile)
        top = functools.reduce(jnp.maximum, [jnp.max(t, axis=1, keepdims=True) for t in tiles])
        expo = [jnp.exp(t - top) for t in tiles]
        row_total = functools.reduce(jnp.add, [jnp.sum(e, axis=1, keepdims=True) for e in expo])
        wanted = pos_cols[here, 0:1]
        heavy = weight_cols[here, 0:1]
        columns = lax.broadcasted_iota(jnp.int32, (GROUP, rows), 1).astype(jnp.float32)
        hit = columns == wanted
        picked = jnp.sum(jnp.where(hit, tiles[0], 0.0), axis=1, keepdims=True)
        ratio = heavy / row_total
        for slot in range(NY):
            value = expo[slot] * ratio
            if slot == 0:
                value = value - jnp.where(hit, heavy, 0.0)
            coeff[slot, here, :] = value.astype(jnp.bfloat16)
        return total + heavy * (top + jnp.log(row_total) - picked)

    total = lax.fori_loop(0, rows // GROUP, soft_rows, jnp.zeros((GROUP, 1), jnp.float32))
    loss_tile[...] = jnp.broadcast_to(jnp.sum(total, axis=0, keepdims=True), loss_tile.shape)

    my_half = pl.ds(pl.multiple_of(core * half, half), half)
    for s in range(1, NY):
        coeff_out[s - 1] = coeff[s, my_half, :]
    coeff_z = [
        send(coeff_out, coeff_beside.at[0], cz_send.at[0], cz_recv.at[0], right_plane),
        send(coeff_out, coeff_beside.at[1], cz_send.at[1], cz_recv.at[1], left_plane),
    ]
    for copy in coeff_z:
        copy.start()

    def spread(buffer, send_sem, recv_sem, mine_at, size, place):
        return [
            send(loss_tile, buffer.at[mine_at], send_sem.at[s - 1], recv_sem.at[mine_at], place(s))
            for s in range(1, size)
        ]

    def collect(buffer, recv_sem, mine_at, size):
        buffer[mine_at] = loss_tile[...]
        for s in range(1, size):
            source = (mine_at + s) % size
            send(loss_tile, buffer.at[source], recv_sem.at[source], recv_sem.at[source], me, 1 - core).wait_recv()
        value = buffer[0]
        for s in range(1, size):
            value = value + buffer[s]
        return value

    loss_along_y = spread(loss_y, ly_send, ly_recv, y, NY, at_y)
    for copy in loss_along_y:
        copy.start()

    landed(count)
    relay(count + 2)
    share(count + 5)

    def query_grad_step(k, carry):
        value = nn_dot(coeff[0], own[k])
        for slot in range(1, NY):
            value = value + nn_dot(coeff[slot], gathered[slot - 1, k])
        query_grad[:, pl.ds(pl.multiple_of(k * CHUNK, CHUNK), CHUNK)] = value
        return carry

    lax.fori_loop(0, count, query_grad_step, 0)

    for copy in coeff_z:
        copy.wait_recv()
    for s in range(1, NY):
        coeff_staged[s - 1] = pick(s, coeff_out[s - 1], coeff_beside[0, s - 1], coeff_beside[1, s - 1])
    coeff_y = [
        send(
            coeff_staged.at[s - 1], coeff_got.at[NY - s - 1], cy_send.at[s - 1], cy_recv.at[NY - s - 1], at_y(s)
        )
        for s in range(1, NY)
    ]
    for copy in coeff_y:
        copy.start()

    landed(count + 1)
    relay(count + 3)
    share(count + 6)
    value = collect(loss_y, ly_recv, y, NY)
    for copy in loss_along_y:
        copy.wait_send()
    loss_tile[...] = value
    loss_along_z = spread(loss_z, lz_send, lz_recv, z, NZ, at_z)
    for copy in loss_along_z:
        copy.start()

    landed(count + 2)
    relay(count + 4)
    share(count + 7)
    for copy in coeff_y:
        copy.wait_recv()
    forward = send(coeff_got, coeff_fwd, cf_send, cf_recv, me, 1 - core)
    forward.start()
    value = collect(loss_z, lz_recv, z, NZ)
    for copy in loss_along_z:
        copy.wait_send()
    loss_tile[...] = value
    loss_along_x = spread(loss_x, lx_send, lx_recv, x, NX, at_x)
    for copy in loss_along_x:
        copy.start()

    landed(count + 3)
    relay(count + 5)
    forward.wait_recv()

    coeff_t[0] = coeff[0].astype(jnp.float32).T.astype(jnp.bfloat16)
    first_half = core == 0
    for slot in range(1, NY):
        got, fwd = coeff_got[slot - 1], coeff_fwd[slot - 1]
        tile = jnp.concatenate([lax.select(first_half, got, fwd), lax.select(first_half, fwd, got)], axis=0)
        tile = tile.astype(jnp.float32).T
        tile = lax.select(linked[slot], tile, jnp.zeros_like(tile))
        coeff_t[slot] = tile.astype(jnp.bfloat16)

    landed(count + 4)
    relay(count + 6)
    value = collect(loss_x, lx_recv, x, NX)
    for copy in loss_along_x:
        copy.wait_send()
    loss_ref[...] = value * (1.0 / (rows * planes * NY))

    def passage_grad_step(k, carry):
        value = nn_dot(coeff_t[0], own[count + k])
        for slot in range(1, NY):
            value = value + nn_dot(coeff_t[slot], gathered[slot - 1, count + k])
        passage_grad[:, pl.ds(pl.multiple_of(k * CHUNK, CHUNK), CHUNK)] = value
        return carry

    landed(count + 5)
    relay(count + 7)
    lax.fori_loop(0, 6, passage_grad_step, 0)
    landed(count + 6)
    passage_grad_step(6, 0)
    landed(count + 7)
    passage_grad_step(7, 0)

    def finish_sends(k, carry):
        for copy in along_z(k):
            copy.wait_send()
        for copy in along_y(k):
            copy.wait_send()
        return carry

    lax.fori_loop(1, 2 * count, finish_sends, 0)
    for copy in first_along_y() + first_along_z() + coeff_z + coeff_y + [swap, forward]:
        copy.wait_send()


def shards(queries, passages, cluster_of_block, positive_row, query_weight):
    rows, width = queries.shape
    count = width // CHUNK
    dma = pltpu.SemaphoreType.DMA
    vmem = pltpu.VMEM
    low, full = jnp.bfloat16, jnp.float32
    tile = (8, 128)
    scratch = [
        pltpu.SMEM(cluster_of_block.shape, jnp.int32),
        vmem((rows // 128, 128), jnp.int32),
        vmem((rows // 128, 128), full),
        vmem((2 * count, rows, CHUNK), full),
        vmem((2 * count, rows, CHUNK), low),
        vmem((2, 2 * count, rows, CHUNK), low),
        vmem((NY - 1, 2 * count, rows, CHUNK), low),
        vmem((NY - 1, 2 * count, rows, CHUNK), low),
        vmem((NY - 1, rows, CHUNK), low),
        vmem((2, NY - 1, rows, CHUNK), low),
        vmem((rows, NY * rows), full),
        vmem((rows, NY * rows), full),
        vmem((NY, rows, rows), low),
        vmem((NY - 1, rows // 2, rows), low),
        vmem((2, NY - 1, rows // 2, rows), low),
        vmem((NY - 1, rows // 2, rows), low),
        vmem((NY - 1, rows // 2, rows), low),
        vmem((NY - 1, rows // 2, rows), low),
        vmem((NY, rows, rows), low),
        vmem((rows, 128), full),
        vmem((rows, 128), full),
        vmem(tile, full),
        vmem((NY,) + tile, full),
        vmem((NZ,) + tile, full),
        vmem((NX,) + tile, full),
        dma((2 * count,)),
        dma((2, 2 * count)),
        dma((2, 2 * count)),
        dma((NY - 1, 2 * count)),
        dma((NY - 1, 2 * count)),
        dma, dma,
        dma((2,)), dma((2,)),
        dma((NY - 1,)), dma((NY - 1,)),
        dma, dma,
        dma((NY,)), dma((NY,)),
        dma((NZ,)), dma((NZ,)),
        dma((NX,)), dma((NX,)),
        dma((2,)), dma((2,)),
        dma((3,)),
    ]
    in_vmem = pl.BlockSpec(memory_space=pltpu.VMEM)
    loss, query_grad, passage_grad = pl.pallas_call(
        kernel,
        out_shape=[
            jax.ShapeDtypeStruct(tile, full),
            vmem((rows, width), full),
            vmem((rows, width), full),
        ],
        in_specs=[pl.BlockSpec(memory_space=pltpu.HBM)] * 5,
        out_specs=[in_vmem, in_vmem, in_vmem],
        scratch_shapes=scratch,
        compiler_params=pltpu.CompilerParams(
            collective_id=0, has_side_effects=True, vmem_limit_bytes=48 * 2**20
        ),
        cost_estimate=pl.CostEstimate(
            flops=6 * NY * rows * rows * width, bytes_accessed=16 * rows * width, transcendentals=NY * rows * rows
        ),
    )(
        *[
            pltpu.with_memory_space_constraint(array, pltpu.HBM)
            for array in (
                queries, passages, cluster_of_block,
                positive_row.reshape(rows // 128, 128), query_weight.reshape(rows // 128, 128),
            )
        ]
    )
    return loss[0, 0], query_grad, passage_grad


def solution(mesh):
    in_specs = (P("dp", "mp"), P("dp", "mp"), P(), P("dp"), P("dp"))
    out_specs = (P(), P("dp", "mp"), P("dp", "mp"))
    return jax.shard_map(shards, mesh=mesh, in_specs=in_specs, out_specs=out_specs, check_vma=False)
```

```python
import functools
import math

import jax
import jax.numpy as jnp
from jax import lax
from jax.experimental import pallas as pl
from jax.experimental.pallas import tpu as pltpu
from jax.sharding import PartitionSpec as P

MESH = pl.DeviceIdType.MESH
NY, NZ, NX = 4, 8, 4
CHUNK = 256
GROUP = 32


def nt_dot(left, right):
    return lax.dot_general(left, right, (((1,), (1,)), ((), ())), preferred_element_type=jnp.float32)


def nn_dot(left, right):
    return jnp.dot(left, right, preferred_element_type=jnp.float32)


def kernel(
    query_hbm, passage_hbm, cluster_hbm, positive_hbm, weight_hbm,
    loss_ref, query_grad, passage_grad,
    cluster, positive, weight, fresh, own, beside, staged, gathered, raw, raw_beside,
    passed, across, ring_out, ring_in,
    score_own, score_other, coeff, coeff_out, coeff_beside, coeff_staged, coeff_got, coeff_fwd, coeff_t, middle_t,
    pos_cols, weight_cols, loss_tile, loss_y, loss_z, loss_x,
    in_sem, z_send, z_recv, y_send, y_recv, s_send, s_recv,
    cz_send, cz_recv, cy_send, cy_recv, cf_send, cf_recv,
    ly_send, ly_recv, lz_send, lz_recv, lx_send, lx_recv, raw_send, raw_recv, small_sem, ring_send, ring_recv, hop_send, hop_recv,
):
    rows, width = query_hbm.shape
    count = width // CHUNK
    half = rows // 2
    planes = NX * NZ
    me = lax.axis_index("dp")
    core = lax.axis_index("mp")
    y = me % NY
    plane = me // NY
    z = plane % NZ
    x = plane // NZ

    def at_y(step):
        return plane * NY + (y + step) % NY

    def at_z(step):
        return (x * NZ + (z + step) % NZ) * NY + y

    def at_x(step):
        return (((x + step) % NX) * NZ + z) * NY + y

    left_plane = ((plane + planes - 1) % planes) * NY + y
    right_plane = ((plane + 1) % planes) * NY + y

    def arriving(k):
        start = pl.multiple_of(k * CHUNK, CHUNK)
        return pltpu.make_async_copy(passage_hbm.at[:, pl.ds(start, CHUNK)], fresh.at[k], in_sem.at[k])

    def arriving_query(k):
        start = pl.multiple_of(k * CHUNK, CHUNK)
        return pltpu.make_async_copy(
            query_hbm.at[:, pl.ds(start, CHUNK)], fresh.at[count + k], in_sem.at[count + k]
        )

    def start_in(k, carry):
        arriving(k).start()
        return carry

    def start_in_query(k, carry):
        arriving_query(k).start()
        return carry

    small = [
        pltpu.make_async_copy(source, target, small_sem.at[i])
        for i, (source, target) in enumerate(
            [(cluster_hbm, cluster), (positive_hbm, positive), (weight_hbm, weight)]
        )
    ]
    arriving(0).start()
    for copy in small:
        copy.start()
    lax.fori_loop(1, count, start_in, 0)
    lax.fori_loop(0, count, start_in_query, 0)

    barrier = pltpu.get_barrier_semaphore()
    peers = [at_y(s) for s in range(1, NY)] + [at_z(s) for s in range(1, NZ)] + [at_x(s) for s in range(1, NX)]
    peers = peers + [left_plane, right_plane]
    for peer in peers:
        pl.semaphore_signal(barrier, inc=1, device_id=(peer, core), device_id_type=MESH)
    pl.semaphore_signal(barrier, inc=1, device_id=(me, 1 - core), device_id_type=MESH)
    pl.semaphore_wait(barrier, len(peers) + 1)

    for copy in small:
        copy.wait()

    last = planes * NY - 1
    mine = cluster[me]
    on_left = cluster[jnp.maximum(me - NY, 0)]
    on_right = cluster[jnp.minimum(me + NY, last)]
    has_left = plane > 0
    has_right = plane < planes - 1
    want_left, want_right, linked = [], [], [None]
    got_left, got_right = [None], [None]
    for step in range(1, NY):
        target = at_y(step)
        theirs = cluster[target]
        want_left.append(has_left & (theirs == on_left))
        want_right.append(has_right & (theirs == on_right))
        from_here = theirs == mine
        from_left = has_left & (cluster[jnp.maximum(target - NY, 0)] == mine)
        from_right = has_right & (cluster[jnp.minimum(target + NY, last)] == mine)
        linked.append(from_here | from_left | from_right)
        got_left.append(from_left)
        got_right.append(from_right)

    def same(step):
        there = me + step
        inside = (there >= 0) & (there <= last)
        return inside & (cluster[jnp.clip(there, 0, last)] == mine)

    near_up, near_down = same(1), same(-1)
    far_up, far_down = same(2), same(-2)
    middle = near_up & near_down & jnp.logical_not(far_up) & jnp.logical_not(far_down)
    top_end = near_down & far_down & jnp.logical_not(same(-3)) & jnp.logical_not(near_up)
    low_end = near_up & far_up & jnp.logical_not(same(3)) & jnp.logical_not(near_down)
    from_beside = [want_left[0] | want_right[0], want_left[2] | want_right[2]]

    def pick(step, here, from_left, from_right):
        return lax.select(
            want_left[step - 1], from_left, lax.select(want_right[step - 1], from_right, here)
        )

    def send(source, target, send_sem, recv_sem, place, where=None):
        return pltpu.make_async_remote_copy(
            src_ref=source, dst_ref=target, send_sem=send_sem, recv_sem=recv_sem,
            device_id=(place, core if where is None else where), device_id_type=MESH,
        )

    def along_z(k):
        return [
            send(own.at[k], beside.at[0, k], z_send.at[0, k], z_recv.at[0, k], right_plane),
            send(own.at[k], beside.at[1, k], z_send.at[1, k], z_recv.at[1, k], left_plane),
        ]

    def along_y(k):
        return [
            send(
                staged.at[s - 1, k], gathered.at[NY - s - 1, k],
                y_send.at[s - 1, k], y_recv.at[NY - s - 1, k], at_y(s),
            )
            for s in range(1, NY)
        ]

    def share(k):
        for copy in along_z(k):
            copy.start()

    def relay(k):
        for copy in along_z(k):
            copy.wait_recv()
        here, from_left, from_right = own[k], beside[0, k], beside[1, k]
        for s in range(1, NY):
            staged[s - 1, k] = pick(s, here, from_left, from_right)
        for copy in along_y(k):
            copy.start()

    def landed(k):
        for copy in along_y(k):
            copy.wait_recv()

    def block(k, slot):
        return own[k] if slot == 0 else gathered[slot - 1, k]

    def add_scores(k, first=False):
        mine_now = own[count + k]
        for slot in range(NY):
            columns = slice(slot * rows, (slot + 1) * rows)
            part = nt_dot(mine_now, block(k, slot))
            if first:
                score_own[:, columns] = part
            else:
                score_own[:, columns] += part

    def cast_passage(k):
        arriving(k).wait()
        own[k] = fresh[k].astype(jnp.bfloat16)

    def first_along_y():
        return [
            send(own.at[0], raw.at[NY - s - 1], y_send.at[s - 1, 0], y_recv.at[NY - s - 1, 0], at_y(s))
            for s in range(1, NY)
        ]

    def first_along_z():
        return [
            send(raw, raw_beside.at[0], raw_send.at[0], raw_recv.at[0], right_plane),
            send(raw, raw_beside.at[1], raw_send.at[1], raw_recv.at[1], left_plane),
        ]

    cast_passage(0)
    for copy in first_along_y():
        copy.start()
    for k in range(1, 4):
        cast_passage(k)
        share(k)

    def cast_rest(k, carry):
        cast_passage(k)
        return carry

    def cast_queries(k, carry):
        arriving_query(k).wait()
        own[count + k] = fresh[count + k].astype(jnp.bfloat16)
        return carry

    lax.fori_loop(4, count, cast_rest, 0)
    lax.fori_loop(0, count, cast_queries, 0)

    for part in range(rows // 128):
        here = slice(part * 128, (part + 1) * 128)
        as_row = positive[part : part + 1, :].astype(jnp.float32)
        pos_cols[here, :] = jnp.broadcast_to(as_row, (128, 128)).T
        weight_cols[here, :] = jnp.broadcast_to(weight[part : part + 1, :], (128, 128)).T

    relay(1)
    share(4)
    for copy in first_along_y():
        copy.wait_recv()
    relay(2)
    share(5)
    landed(1)
    add_scores(1, first=True)

    part = count // 2
    hop_place = [
        jnp.where(y == NY - 1, right_plane, left_plane),
        jnp.where(y == 0, left_plane, right_plane),
    ]
    wraps = [y == NY - 1, y == 0]
    steps = [1, NY - 1]

    def ring(way, q):
        return send(
            ring_out.at[way, q], ring_in.at[way, q], ring_send.at[way, q], ring_recv.at[way, q], at_y(steps[way])
        )

    def hop(way, j):
        return send(
            passed.at[way, j], across.at[way, j], hop_send.at[way, j], hop_recv.at[way, j], hop_place[way]
        )

    def query_chunk(way, q):
        return count + (q + part) % count if way == 0 else count + q

    def ring_first(q):
        for k in (q, q + part):
            for copy in along_z(count + k):
                copy.wait_recv()
        for way in range(2):
            k = query_chunk(way, q)
            ring_out[way, q] = pick(steps[way], own[k], beside[0, k], beside[1, k])
            ring(way, q).start()

    def ring_landed(q):
        for way in range(2):
            ring(way, q).wait_recv()

    def pass_second(j):
        for way in range(2):
            passed[way, j] = lax.select(middle, ring_in[way, j], own[query_chunk(way, part + j)])

            @pl.when(wraps[way])
            def _():
                hop(way, j).start()

    def ring_second(j):
        q = part + j
        for way in range(2):
            k = query_chunk(way, q)
            ring_out[way, q] = pick(steps[way], passed[way, j], beside[0, k], beside[1, k])

            @pl.when(wraps[way])
            def _():
                hop(way, j).wait_recv()
                ring_out[way, q] = lax.select(from_beside[way], across[way, j], passed[way, j])

            ring(way, q).start()

    def pass_last(j):
        for way in range(2):
            k = query_chunk(way, part + j)
            terms = nn_dot(middle_t[way], own[k]) + nn_dot(middle_t[2 + way], ring_in[way, part + j])
            passed[way, part + j] = lax.select(middle, terms.astype(jnp.bfloat16), ring_in[way, j])
            hop(way, part + j).start()

    def ring_last(j):
        q = count + j
        for way in range(2):
            hop(way, part + j).wait_recv()
            ring_out[way, q] = lax.select(from_beside[way], across[way, part + j], passed[way, part + j])
            ring(way, q).start()

    def passage_step(k, shares):
        relay(k)
        for share_now in shares:
            share(share_now)
        landed(k - 1)
        add_scores(k - 1)

    passage_step(3, [6])
    for copy in first_along_z():
        copy.start()
    passage_step(4, [7])
    for k in range(5, count):
        passage_step(k, [count + k - 5, count + part + k - 5])
    for copy in first_along_z():
        copy.wait_recv()
    for slot in range(1, NY):
        gathered[slot - 1, 0] = lax.select(
            got_left[slot], raw_beside[0, slot - 1],
            lax.select(got_right[slot], raw_beside[1, slot - 1], raw[slot - 1]),
        )
    add_scores(0)
    share(count + part - 1)
    share(2 * count - 1)
    ring_first(0)
    landed(count - 1)
    ring_first(1)
    add_scores(count - 1)
    swap = send(score_own, score_other, s_send, s_recv, me, 1 - core)
    swap.start()
    ring_first(2)
    swap.wait_recv()

    scale = 3.0 / math.sqrt(2 * width)

    def soft_rows(group, total):
        here = pl.ds(pl.multiple_of(group * GROUP, GROUP), GROUP)
        tiles = []
        for slot in range(NY):
            columns = slice(slot * rows, (slot + 1) * rows)
            tile = (score_own[here, columns] + score_other[here, columns]) * scale
            if slot > 0:
                tile = lax.select(linked[slot], tile, jnp.full_like(tile, -1e30))
            tiles.append(tile)
        top = functools.reduce(jnp.maximum, [jnp.max(t, axis=1, keepdims=True) for t in tiles])
        expo = [jnp.exp(t - top) for t in tiles]
        row_total = functools.reduce(jnp.add, [jnp.sum(e, axis=1, keepdims=True) for e in expo])
        wanted = pos_cols[here, 0:1]
        heavy = weight_cols[here, 0:1]
        columns = lax.broadcasted_iota(jnp.int32, (GROUP, rows), 1).astype(jnp.float32)
        hit = columns == wanted
        picked = jnp.sum(jnp.where(hit, tiles[0], 0.0), axis=1, keepdims=True)
        ratio = heavy / row_total
        for slot in range(NY):
            value = expo[slot] * ratio
            if slot == 0:
                value = value - jnp.where(hit, heavy, 0.0)
            coeff[slot, here, :] = value.astype(jnp.bfloat16)
        return total + heavy * (top + jnp.log(row_total) - picked)

    total = lax.fori_loop(0, rows // GROUP, soft_rows, jnp.zeros((GROUP, 1), jnp.float32))
    loss_tile[...] = jnp.broadcast_to(jnp.sum(total, axis=0, keepdims=True), loss_tile.shape)

    my_half = pl.ds(pl.multiple_of(core * half, half), half)
    for s in range(1, NY):
        coeff_out[s - 1] = coeff[s, my_half, :]
    coeff_z = [
        send(coeff_out, coeff_beside.at[0], cz_send.at[0], cz_recv.at[0], right_plane),
        send(coeff_out, coeff_beside.at[1], cz_send.at[1], cz_recv.at[1], left_plane),
    ]
    for copy in coeff_z:
        copy.start()

    def spread(buffer, send_sem, recv_sem, mine_at, size, place):
        return [
            send(loss_tile, buffer.at[mine_at], send_sem.at[s - 1], recv_sem.at[mine_at], place(s))
            for s in range(1, size)
        ]

    def collect(buffer, recv_sem, mine_at, size):
        buffer[mine_at] = loss_tile[...]
        for s in range(1, size):
            source = (mine_at + s) % size
            send(loss_tile, buffer.at[source], recv_sem.at[source], recv_sem.at[source], me, 1 - core).wait_recv()
        value = buffer[0]
        for s in range(1, size):
            value = value + buffer[s]
        return value

    loss_along_y = spread(loss_y, ly_send, ly_recv, y, NY, at_y)
    for copy in loss_along_y:
        copy.start()

    ring_first(3)
    for j in range(2):
        ring_landed(j)
        pass_second(j)

    def query_grad_step(k, carry):
        value = nn_dot(coeff[0], own[k])
        for slot in range(1, NY):
            value = value + nn_dot(coeff[slot], gathered[slot - 1, k])
        query_grad[:, pl.ds(pl.multiple_of(k * CHUNK, CHUNK), CHUNK)] = value
        return carry

    lax.fori_loop(0, count, query_grad_step, 0)

    for copy in coeff_z:
        copy.wait_recv()
    for place, (s, tile) in enumerate([(1, 1), (1, 2), (2, 2), (3, 3), (3, 2)]):
        coeff_staged[place] = pick(s, coeff_out[tile - 1], coeff_beside[0, tile - 1], coeff_beside[1, tile - 1])
    coeff_y = [
        send(coeff_staged.at[0:2], coeff_got.at[3:5], cy_send.at[0], cy_recv.at[2], at_y(1)),
        send(coeff_staged.at[2], coeff_got.at[2], cy_send.at[1], cy_recv.at[1], at_y(2)),
        send(coeff_staged.at[3:5], coeff_got.at[0:2], cy_send.at[2], cy_recv.at[0], at_y(3)),
    ]
    for copy in coeff_y:
        copy.start()

    ring_second(0)
    ring_landed(2)
    pass_second(2)
    ring_second(1)
    ring_landed(3)
    pass_second(3)
    value = collect(loss_y, ly_recv, y, NY)
    for copy in loss_along_y:
        copy.wait_send()
    loss_tile[...] = value
    loss_along_z = spread(loss_z, lz_send, lz_recv, z, NZ, at_z)
    for copy in loss_along_z:
        copy.start()
    ring_second(2)
    for copy in coeff_y:
        copy.wait_recv()
    forward = send(coeff_got, coeff_fwd, cf_send, cf_recv, me, 1 - core)
    forward.start()
    ring_second(3)

    def turned(tile):
        return tile.astype(jnp.float32).T

    coeff_t[0] = turned(coeff[0]).astype(jnp.bfloat16)
    middle_t[0] = turned(coeff[1]).astype(jnp.bfloat16)
    middle_t[1] = turned(coeff[3]).astype(jnp.bfloat16)
    forward.wait_recv()
    first_half = core == 0

    def whole(place):
        got, fwd = coeff_got[place], coeff_fwd[place]
        return turned(
            jnp.concatenate([lax.select(first_half, got, fwd), lax.select(first_half, fwd, got)], axis=0)
        )

    middle_t[2] = whole(4).astype(jnp.bfloat16)
    middle_t[3] = whole(1).astype(jnp.bfloat16)
    ring_landed(4)
    pass_last(0)
    ring_landed(5)
    pass_last(1)
    for slot, place in ((1, 0), (2, 2), (3, 3)):
        tile = whole(place)
        coeff_t[slot] = lax.select(linked[slot], tile, jnp.zeros_like(tile)).astype(jnp.bfloat16)
    ring_last(0)
    ring_landed(6)
    pass_last(2)
    ring_last(1)
    ring_landed(7)
    pass_last(3)
    value = collect(loss_z, lz_recv, z, NZ)
    for copy in loss_along_z:
        copy.wait_send()
    loss_tile[...] = value
    loss_along_x = spread(loss_x, lx_send, lx_recv, x, NX, at_x)
    for copy in loss_along_x:
        copy.start()
    ring_last(2)
    ring_last(3)

    def passage_grad_chunk(k, start):
        j = k % part
        up, down = ring_in[0, (k + part) % count], ring_in[1, k]
        far = ring_in[1 if start else 0, count + j]
        relayed = ring_in[1 if start else 0, part + j]
        near_end, far_end = (low_end, top_end) if start else (top_end, low_end)
        done = ring_in[0 if start else 1, count + j].astype(jnp.float32)
        from_up = nn_dot(coeff_t[NY - 1], up)
        from_down = nn_dot(coeff_t[1], down)
        if start:
            from_up = lax.select(far_end, done, from_up)
        else:
            from_down = lax.select(far_end, done, from_down)
        opposite = nn_dot(coeff_t[2], lax.select(near_end, relayed, far))
        opposite = lax.select(far_end, jnp.zeros_like(opposite), opposite)
        value = nn_dot(coeff_t[0], own[count + k]) + from_up + from_down + opposite
        passage_grad[:, k * CHUNK : (k + 1) * CHUNK] = value

    for j in range(part):
        ring_landed(count + j)
        passage_grad_chunk(j, True)
        passage_grad_chunk(part + j, False)
        if j == 0:
            value = collect(loss_x, lx_recv, x, NX)
            for copy in loss_along_x:
                copy.wait_send()
            loss_ref[...] = value * (1.0 / (rows * planes * NY))

    def finish_shares(k, carry):
        for copy in along_z(k):
            copy.wait_send()
        return carry

    def finish_chunks(k, carry):
        for copy in along_y(k):
            copy.wait_send()
        return carry

    def finish_ring(q, carry):
        for way in range(2):
            ring(way, q).wait_send()
        return carry

    def finish_hops(j, carry):
        for way in range(2):
            hop(way, j).wait_send()
        return carry

    lax.fori_loop(1, 2 * count, finish_shares, 0)
    lax.fori_loop(1, count, finish_chunks, 0)
    lax.fori_loop(0, count + part, finish_ring, 0)
    for way in range(2):

        @pl.when(wraps[way])
        def _():
            for j in range(part):
                hop(way, j).wait_send()

    lax.fori_loop(part, count, finish_hops, 0)
    for copy in first_along_y() + first_along_z() + coeff_z + coeff_y + [swap, forward]:
        copy.wait_send()


def shards(queries, passages, cluster_of_block, positive_row, query_weight):
    rows, width = queries.shape
    count = width // CHUNK
    dma = pltpu.SemaphoreType.DMA
    vmem = pltpu.VMEM
    low, full = jnp.bfloat16, jnp.float32
    tile = (8, 128)
    slots = count + count // 2
    scratch = [
        pltpu.SMEM(cluster_of_block.shape, jnp.int32),
        vmem((rows // 128, 128), jnp.int32),
        vmem((rows // 128, 128), full),
        vmem((2 * count, rows, CHUNK), full),
        vmem((2 * count, rows, CHUNK), low),
        vmem((2, 2 * count, rows, CHUNK), low),
        vmem((NY - 1, count, rows, CHUNK), low),
        vmem((NY - 1, count, rows, CHUNK), low),
        vmem((NY - 1, rows, CHUNK), low),
        vmem((2, NY - 1, rows, CHUNK), low),
        vmem((2, count, rows, CHUNK), low),
        vmem((2, count, rows, CHUNK), low),
        vmem((2, slots, rows, CHUNK), low),
        vmem((2, slots, rows, CHUNK), low),
        vmem((rows, NY * rows), full),
        vmem((rows, NY * rows), full),
        vmem((NY, rows, rows), low),
        vmem((NY - 1, rows // 2, rows), low),
        vmem((2, NY - 1, rows // 2, rows), low),
        vmem((NY + 1, rows // 2, rows), low),
        vmem((NY + 1, rows // 2, rows), low),
        vmem((NY + 1, rows // 2, rows), low),
        vmem((NY, rows, rows), low),
        vmem((NY, rows, rows), low),
        vmem((rows, 128), full),
        vmem((rows, 128), full),
        vmem(tile, full),
        vmem((NY,) + tile, full),
        vmem((NZ,) + tile, full),
        vmem((NX,) + tile, full),
        dma((2 * count,)),
        dma((2, 2 * count)),
        dma((2, 2 * count)),
        dma((NY - 1, count)),
        dma((NY - 1, count)),
        dma, dma,
        dma((2,)), dma((2,)),
        dma((NY - 1,)), dma((NY - 1,)),
        dma, dma,
        dma((NY,)), dma((NY,)),
        dma((NZ,)), dma((NZ,)),
        dma((NX,)), dma((NX,)),
        dma((2,)), dma((2,)),
        dma((3,)),
        dma((2, slots)), dma((2, slots)),
        dma((2, count)), dma((2, count)),
    ]
    in_vmem = pl.BlockSpec(memory_space=pltpu.VMEM)
    loss, query_grad, passage_grad = pl.pallas_call(
        kernel,
        out_shape=[
            jax.ShapeDtypeStruct(tile, full),
            vmem((rows, width), full),
            vmem((rows, width), full),
        ],
        in_specs=[pl.BlockSpec(memory_space=pltpu.HBM)] * 5,
        out_specs=[in_vmem, in_vmem, in_vmem],
        scratch_shapes=scratch,
        compiler_params=pltpu.CompilerParams(
            collective_id=0, has_side_effects=True, vmem_limit_bytes=48 * 2**20
        ),
        cost_estimate=pl.CostEstimate(
            flops=6 * NY * rows * rows * width, bytes_accessed=16 * rows * width, transcendentals=NY * rows * rows
        ),
    )(
        *[
            pltpu.with_memory_space_constraint(array, pltpu.HBM)
            for array in (
                queries, passages, cluster_of_block,
                positive_row.reshape(rows // 128, 128), query_weight.reshape(rows // 128, 128),
            )
        ]
    )
    return loss[0, 0], query_grad, passage_grad


def solution(mesh):
    in_specs = (P("dp", "mp"), P("dp", "mp"), P(), P("dp"), P("dp"))
    out_specs = (P(), P("dp", "mp"), P("dp", "mp"))
    return jax.shard_map(shards, mesh=mesh, in_specs=in_specs, out_specs=out_specs, check_vma=False)
```

```python
import functools
import math

import jax
import jax.numpy as jnp
from jax import lax
from jax.experimental import pallas as pl
from jax.experimental.pallas import tpu as pltpu
from jax.sharding import PartitionSpec as P

MESH = pl.DeviceIdType.MESH
NY, NZ, NX = 4, 8, 4
CHUNK = 256
GROUP = 32


def nt_dot(left, right):
    return lax.dot_general(left, right, (((1,), (1,)), ((), ())), preferred_element_type=jnp.float32)


def nn_dot(left, right):
    return jnp.dot(left, right, preferred_element_type=jnp.float32)


def kernel(
    query_hbm, passage_hbm, cluster_hbm, positive_hbm, weight_hbm,
    loss_ref, query_grad, passage_grad,
    cluster, positive, weight, fresh, own, beside, staged, gathered, raw, raw_beside,
    passed, across, ring_out, ring_in,
    score_own, score_other, coeff, coeff_out, coeff_beside, coeff_staged, coeff_got, coeff_fwd, coeff_t, middle_t,
    pos_cols, weight_cols, loss_tile, loss_y, loss_z, loss_x,
    in_sem, z_send, z_recv, y_send, y_recv, s_send, s_recv,
    cz_send, cz_recv, cy_send, cy_recv, cf_send, cf_recv,
    ly_send, ly_recv, lz_send, lz_recv, lx_send, lx_recv, raw_send, raw_recv, small_sem, ring_send, ring_recv, hop_send, hop_recv,
):
    rows, width = query_hbm.shape
    count = width // CHUNK
    half = rows // 2
    planes = NX * NZ
    me = lax.axis_index("dp")
    core = lax.axis_index("mp")
    y = me % NY
    plane = me // NY
    z = plane % NZ
    x = plane // NZ

    def at_y(step):
        return plane * NY + (y + step) % NY

    def at_z(step):
        return (x * NZ + (z + step) % NZ) * NY + y

    def at_x(step):
        return (((x + step) % NX) * NZ + z) * NY + y

    left_plane = ((plane + planes - 1) % planes) * NY + y
    right_plane = ((plane + 1) % planes) * NY + y
    one_way = [jnp.where(y + s < NY, right_plane, left_plane) for s in range(1, NY)]
    other_way = [jnp.where(y + s < NY, left_plane, right_plane) for s in range(1, NY)]

    def arriving(k):
        start = pl.multiple_of(k * CHUNK, CHUNK)
        return pltpu.make_async_copy(passage_hbm.at[:, pl.ds(start, CHUNK)], fresh.at[k], in_sem.at[k])

    def arriving_query(k):
        start = pl.multiple_of(k * CHUNK, CHUNK)
        return pltpu.make_async_copy(
            query_hbm.at[:, pl.ds(start, CHUNK)], fresh.at[count + k], in_sem.at[count + k]
        )

    def start_in(k, carry):
        arriving(k).start()
        return carry

    def start_in_query(k, carry):
        arriving_query(k).start()
        return carry

    small = [
        pltpu.make_async_copy(source, target, small_sem.at[i])
        for i, (source, target) in enumerate(
            [(cluster_hbm, cluster), (positive_hbm, positive), (weight_hbm, weight)]
        )
    ]
    arriving(0).start()
    for copy in small:
        copy.start()
    lax.fori_loop(1, count, start_in, 0)
    lax.fori_loop(0, count, start_in_query, 0)

    barrier = pltpu.get_barrier_semaphore()
    peers = [at_y(s) for s in range(1, NY)] + [at_z(s) for s in range(1, NZ)] + [at_x(s) for s in range(1, NX)]
    peers = peers + [left_plane, right_plane]
    for peer in peers:
        pl.semaphore_signal(barrier, inc=1, device_id=(peer, core), device_id_type=MESH)
    pl.semaphore_signal(barrier, inc=1, device_id=(me, 1 - core), device_id_type=MESH)
    pl.semaphore_wait(barrier, len(peers) + 1)

    for copy in small:
        copy.wait()

    last = planes * NY - 1
    mine = cluster[me]
    on_left = cluster[jnp.maximum(me - NY, 0)]
    on_right = cluster[jnp.minimum(me + NY, last)]
    has_left = plane > 0
    has_right = plane < planes - 1
    want_left, want_right, linked = [], [], [None]
    got_beside = [None]
    for step in range(1, NY):
        target = at_y(step)
        theirs = cluster[target]
        want_left.append(has_left & (theirs == on_left))
        want_right.append(has_right & (theirs == on_right))
        from_here = theirs == mine
        from_left = has_left & (cluster[jnp.maximum(target - NY, 0)] == mine)
        from_right = has_right & (cluster[jnp.minimum(target + NY, last)] == mine)
        linked.append(from_here | from_left | from_right)
        got_beside.append(from_left | from_right)

    def same(step):
        there = me + step
        inside = (there >= 0) & (there <= last)
        return inside & (cluster[jnp.clip(there, 0, last)] == mine)

    near_up, near_down = same(1), same(-1)
    far_up, far_down = same(2), same(-2)
    middle = near_up & near_down & jnp.logical_not(far_up) & jnp.logical_not(far_down)
    top_end = near_down & far_down & jnp.logical_not(same(-3)) & jnp.logical_not(near_up)
    low_end = near_up & far_up & jnp.logical_not(same(3)) & jnp.logical_not(near_down)
    from_beside = [want_left[0] | want_right[0], want_left[2] | want_right[2]]

    def pick(step, here, from_left, from_right):
        return lax.select(
            want_left[step - 1], from_left, lax.select(want_right[step - 1], from_right, here)
        )

    def send(source, target, send_sem, recv_sem, place, where=None):
        return pltpu.make_async_remote_copy(
            src_ref=source, dst_ref=target, send_sem=send_sem, recv_sem=recv_sem,
            device_id=(place, core if where is None else where), device_id_type=MESH,
        )

    def along_z(k):
        return [
            send(own.at[k], beside.at[0, k], z_send.at[0, k], z_recv.at[0, k], right_plane),
            send(own.at[k], beside.at[1, k], z_send.at[1, k], z_recv.at[1, k], left_plane),
        ]

    def along_y(k):
        return [
            send(
                staged.at[s - 1, k], gathered.at[NY - s - 1, k],
                y_send.at[s - 1, k], y_recv.at[NY - s - 1, k], at_y(s),
            )
            for s in range(1, NY)
        ]

    def share(k):
        for copy in along_z(k):
            copy.start()

    def relay(k):
        for copy in along_z(k):
            copy.wait_recv()
        here, from_left, from_right = own[k], beside[0, k], beside[1, k]
        for s in range(1, NY):
            staged[s - 1, k] = pick(s, here, from_left, from_right)
        for copy in along_y(k):
            copy.start()

    def landed(k):
        for copy in along_y(k):
            copy.wait_recv()

    def block(k, slot):
        return own[k] if slot == 0 else gathered[slot - 1, k]

    def add_scores(k, first=False):
        mine_now = own[count + k]
        for slot in range(NY):
            columns = slice(slot * rows, (slot + 1) * rows)
            part = nt_dot(mine_now, block(k, slot))
            if first:
                score_own[:, columns] = part
            else:
                score_own[:, columns] += part

    def cast_passage(k):
        arriving(k).wait()
        own[k] = fresh[k].astype(jnp.bfloat16)

    def first_along_y():
        return [
            send(own.at[0], raw.at[NY - s - 1], y_send.at[s - 1, 0], y_recv.at[NY - s - 1, 0], at_y(s))
            for s in range(1, NY)
        ]

    def first_along_z():
        return [
            send(raw.at[s - 1], raw_beside.at[s - 1], raw_send.at[s - 1], raw_recv.at[s - 1], one_way[s - 1])
            for s in range(1, NY)
        ]

    cast_passage(0)
    for copy in first_along_y():
        copy.start()
    for k in range(1, 4):
        cast_passage(k)
        share(k)

    def cast_rest(k, carry):
        cast_passage(k)
        return carry

    def cast_queries(k, carry):
        arriving_query(k).wait()
        own[count + k] = fresh[count + k].astype(jnp.bfloat16)
        return carry

    lax.fori_loop(4, count, cast_rest, 0)
    lax.fori_loop(0, count, cast_queries, 0)

    for part in range(rows // 128):
        here = slice(part * 128, (part + 1) * 128)
        as_row = positive[part : part + 1, :].astype(jnp.float32)
        pos_cols[here, :] = jnp.broadcast_to(as_row, (128, 128)).T
        weight_cols[here, :] = jnp.broadcast_to(weight[part : part + 1, :], (128, 128)).T

    relay(1)
    share(4)
    for copy in first_along_y():
        copy.wait_recv()
    relay(2)
    share(5)
    landed(1)
    add_scores(1, first=True)

    part = count // 2
    hop_place = [
        jnp.where(y == NY - 1, right_plane, left_plane),
        jnp.where(y == 0, left_plane, right_plane),
    ]
    wraps = [y == NY - 1, y == 0]
    steps = [1, NY - 1]

    def ring(way, q):
        return send(
            ring_out.at[way, q], ring_in.at[way, q], ring_send.at[way, q], ring_recv.at[way, q], at_y(steps[way])
        )

    def hop(way, j, relayed=False):
        source = ring_in.at[way, j - part] if relayed else passed.at[way, j]
        return send(source, across.at[way, j], hop_send.at[way, j], hop_recv.at[way, j], hop_place[way])

    late_place = [right_plane, left_plane]
    late_columns = [y == 0, y == NY - 1]
    late_wanted = [near_down, near_up]

    def late(way, j):
        return send(
            ring_in.at[way, part + j], across.at[way, j], hop_send.at[way, j], hop_recv.at[way, j], late_place[way]
        )

    def query_chunk(way, q):
        return count + (q + part) % count if way == 0 else count + q

    def ring_first(q):
        for k in (q, q + part):
            for copy in along_z(count + k):
                copy.wait_recv()
        for way in range(2):
            k = query_chunk(way, q)
            ring_out[way, q] = pick(steps[way], own[k], beside[0, k], beside[1, k])
            ring(way, q).start()

    def ring_landed(q):
        for way in range(2):
            ring(way, q).wait_recv()

    def pass_relayed(j):
        for way in range(2):

            @pl.when(jnp.logical_not(wraps[way]))
            def _():
                hop(way, part + j, True).start()

    def ring_second(j):
        q = part + j
        for way in range(2):
            k = query_chunk(way, q)
            here = lax.select(middle, ring_in[way, j], own[k])
            s = steps[way] - 1
            inside = jnp.logical_not(wraps[way])
            here = lax.select(inside & want_right[s], beside[1, k], here)
            ring_out[way, q] = lax.select(inside & want_left[s], beside[0, k], here)
            ring(way, q).start()

    def last_content(way, j):
        k = query_chunk(way, part + j)
        terms = nn_dot(middle_t[way], own[k]) + nn_dot(middle_t[2 + way], ring_in[way, part + j])
        passed[way, part + j] = lax.select(middle, terms.astype(jnp.bfloat16), ring_in[way, j])

    def begin_last(j):
        for way in range(2):

            @pl.when(late_columns[way])
            def _():
                late(way, j).start()

        for way in range(2):

            @pl.when(wraps[way])
            def _():
                last_content(way, j)
                hop(way, part + j).start()

    def finish_last(j):
        for way in range(2):

            @pl.when(late_columns[way])
            def _():
                late(way, j).wait()
                ring_in[way, part + j] = lax.select(late_wanted[way], across[way, j], ring_in[way, part + j])

        for way in range(2):

            @pl.when(jnp.logical_not(wraps[way]))
            def _():
                last_content(way, j)

    def ring_last(j):
        q = count + j
        for way in range(2):
            hop(way, part + j).wait_recv()
            ring_out[way, q] = lax.select(from_beside[way], across[way, part + j], passed[way, part + j])
            ring(way, q).start()

    def passage_step(k, shares):
        relay(k)
        for share_now in shares:
            share(share_now)
        landed(k - 1)
        add_scores(k - 1)

    passage_step(3, [6])
    for copy in first_along_z():
        copy.start()
    passage_step(4, [7])
    for k in range(5, count):
        passage_step(k, [count + k - 5, count + part + k - 5])
    for copy in first_along_z():
        copy.wait_recv()
    for slot in range(1, NY):
        gathered[slot - 1, 0] = lax.select(got_beside[slot], raw_beside[slot - 1], raw[slot - 1])
    add_scores(0)
    share(count + part - 1)
    share(2 * count - 1)
    ring_first(0)
    landed(count - 1)
    ring_first(1)
    add_scores(count - 1)
    swap = send(score_own, score_other, s_send, s_recv, me, 1 - core)
    swap.start()
    ring_first(2)
    swap.wait_recv()

    scale = 3.0 / math.sqrt(2 * width)

    def soft_rows(group, total):
        here = pl.ds(pl.multiple_of(group * GROUP, GROUP), GROUP)
        tiles = []
        for slot in range(NY):
            columns = slice(slot * rows, (slot + 1) * rows)
            tile = (score_own[here, columns] + score_other[here, columns]) * scale
            if slot > 0:
                tile = lax.select(linked[slot], tile, jnp.full_like(tile, -1e30))
            tiles.append(tile)
        top = functools.reduce(jnp.maximum, [jnp.max(t, axis=1, keepdims=True) for t in tiles])
        expo = [jnp.exp(t - top) for t in tiles]
        row_total = functools.reduce(jnp.add, [jnp.sum(e, axis=1, keepdims=True) for e in expo])
        wanted = pos_cols[here, 0:1]
        heavy = weight_cols[here, 0:1]
        columns = lax.broadcasted_iota(jnp.int32, (GROUP, rows), 1).astype(jnp.float32)
        hit = columns == wanted
        picked = jnp.sum(jnp.where(hit, tiles[0], 0.0), axis=1, keepdims=True)
        ratio = heavy / row_total
        for slot in range(NY):
            value = expo[slot] * ratio
            if slot == 0:
                value = value - jnp.where(hit, heavy, 0.0)
            coeff[slot, here, :] = value.astype(jnp.bfloat16)
        return total + heavy * (top + jnp.log(row_total) - picked)

    total = lax.fori_loop(0, rows // GROUP, soft_rows, jnp.zeros((GROUP, 1), jnp.float32))
    loss_tile[...] = jnp.broadcast_to(jnp.sum(total, axis=0, keepdims=True), loss_tile.shape)

    my_half = pl.ds(pl.multiple_of(core * half, half), half)
    for s in range(1, NY):
        coeff_out[s - 1] = coeff[s, my_half, :]
    coeff_z = [
        send(coeff_out.at[s - 1], coeff_beside.at[s - 1], cz_send.at[s - 1], cz_recv.at[s - 1], other_way[s - 1])
        for s in range(1, NY)
    ]
    for copy in coeff_z:
        copy.start()

    def spread(buffer, send_sem, recv_sem, mine_at, size, place):
        return [
            send(loss_tile, buffer.at[mine_at], send_sem.at[s - 1], recv_sem.at[mine_at], place(s))
            for s in range(1, size)
        ]

    def collect(buffer, recv_sem, mine_at, size):
        buffer[mine_at] = loss_tile[...]
        for s in range(1, size):
            source = (mine_at + s) % size
            send(loss_tile, buffer.at[source], recv_sem.at[source], recv_sem.at[source], me, 1 - core).wait_recv()
        value = buffer[0]
        for s in range(1, size):
            value = value + buffer[s]
        return value

    loss_along_y = spread(loss_y, ly_send, ly_recv, y, NY, at_y)
    for copy in loss_along_y:
        copy.start()

    ring_first(3)
    for j in range(2):
        ring_landed(j)
        pass_relayed(j)

    def query_grad_step(k, carry):
        value = nn_dot(coeff[0], own[k])
        for slot in range(1, NY):
            value = value + nn_dot(coeff[slot], gathered[slot - 1, k])
        query_grad[:, pl.ds(pl.multiple_of(k * CHUNK, CHUNK), CHUNK)] = value
        return carry

    lax.fori_loop(0, count, query_grad_step, 0)

    for copy in coeff_z:
        copy.wait_recv()
    for place, (s, tile) in enumerate([(1, 1), (1, 2), (2, 2), (3, 3), (3, 2)]):
        coeff_staged[place] = lax.select(
            want_left[s - 1] | want_right[s - 1], coeff_beside[tile - 1], coeff_out[tile - 1]
        )
    coeff_y = [
        send(coeff_staged.at[0:2], coeff_got.at[3:5], cy_send.at[0], cy_recv.at[2], at_y(1)),
        send(coeff_staged.at[2], coeff_got.at[2], cy_send.at[1], cy_recv.at[1], at_y(2)),
        send(coeff_staged.at[3:5], coeff_got.at[0:2], cy_send.at[2], cy_recv.at[0], at_y(3)),
    ]
    for copy in coeff_y:
        copy.start()

    ring_second(0)
    ring_landed(2)
    pass_relayed(2)
    ring_second(1)
    ring_landed(3)
    pass_relayed(3)
    value = collect(loss_y, ly_recv, y, NY)
    for copy in loss_along_y:
        copy.wait_send()
    loss_tile[...] = value
    loss_along_z = spread(loss_z, lz_send, lz_recv, z, NZ, at_z)
    for copy in loss_along_z:
        copy.start()
    ring_second(2)
    for copy in coeff_y:
        copy.wait_recv()
    forward = send(coeff_got, coeff_fwd, cf_send, cf_recv, me, 1 - core)
    forward.start()
    ring_second(3)

    def turned(tile):
        return tile.astype(jnp.float32).T

    coeff_t[0] = turned(coeff[0]).astype(jnp.bfloat16)
    middle_t[0] = turned(coeff[1]).astype(jnp.bfloat16)
    middle_t[1] = turned(coeff[3]).astype(jnp.bfloat16)
    forward.wait_recv()
    first_half = core == 0

    def whole(place):
        got, fwd = coeff_got[place], coeff_fwd[place]
        return turned(
            jnp.concatenate([lax.select(first_half, got, fwd), lax.select(first_half, fwd, got)], axis=0)
        )

    middle_t[2] = whole(4).astype(jnp.bfloat16)
    middle_t[3] = whole(1).astype(jnp.bfloat16)
    ring_landed(4)
    begin_last(0)
    for slot, place in ((1, 0), (2, 2), (3, 3)):
        tile = whole(place)
        coeff_t[slot] = lax.select(linked[slot], tile, jnp.zeros_like(tile)).astype(jnp.bfloat16)
    ring_landed(5)
    begin_last(1)
    finish_last(0)
    ring_last(0)
    ring_landed(6)
    begin_last(2)
    finish_last(1)
    ring_last(1)
    ring_landed(7)
    begin_last(3)
    finish_last(2)
    ring_last(2)
    value = collect(loss_z, lz_recv, z, NZ)
    for copy in loss_along_z:
        copy.wait_send()
    loss_tile[...] = value
    loss_along_x = spread(loss_x, lx_send, lx_recv, x, NX, at_x)
    for copy in loss_along_x:
        copy.start()
    finish_last(3)
    ring_last(3)

    def passage_grad_chunk(k, start):
        j = k % part
        up, down = ring_in[0, (k + part) % count], ring_in[1, k]
        far = ring_in[1 if start else 0, count + j]
        relayed = ring_in[1 if start else 0, part + j]
        near_end, far_end = (low_end, top_end) if start else (top_end, low_end)
        done = ring_in[0 if start else 1, count + j].astype(jnp.float32)
        from_up = nn_dot(coeff_t[NY - 1], up)
        from_down = nn_dot(coeff_t[1], down)
        if start:
            from_up = lax.select(far_end, done, from_up)
        else:
            from_down = lax.select(far_end, done, from_down)
        opposite = nn_dot(coeff_t[2], lax.select(near_end, relayed, far))
        opposite = lax.select(far_end, jnp.zeros_like(opposite), opposite)
        value = nn_dot(coeff_t[0], own[count + k]) + from_up + from_down + opposite
        passage_grad[:, k * CHUNK : (k + 1) * CHUNK] = value

    for j in range(part):
        ring_landed(count + j)
        passage_grad_chunk(j, True)
        passage_grad_chunk(part + j, False)
        if j == 0:
            value = collect(loss_x, lx_recv, x, NX)
            for copy in loss_along_x:
                copy.wait_send()
            loss_ref[...] = value * (1.0 / (rows * planes * NY))

    def finish_shares(k, carry):
        for copy in along_z(k):
            copy.wait_send()
        return carry

    def finish_chunks(k, carry):
        for copy in along_y(k):
            copy.wait_send()
        return carry

    def finish_ring(q, carry):
        for way in range(2):
            ring(way, q).wait_send()
        return carry

    def finish_hops(j, carry):
        for way in range(2):
            hop(way, j).wait_send()
        return carry

    lax.fori_loop(1, 2 * count, finish_shares, 0)
    lax.fori_loop(1, count, finish_chunks, 0)
    lax.fori_loop(0, count + part, finish_ring, 0)
    lax.fori_loop(part, count, finish_hops, 0)
    for copy in first_along_y() + first_along_z() + coeff_z + coeff_y + [swap, forward]:
        copy.wait_send()


def shards(queries, passages, cluster_of_block, positive_row, query_weight):
    rows, width = queries.shape
    count = width // CHUNK
    dma = pltpu.SemaphoreType.DMA
    vmem = pltpu.VMEM
    low, full = jnp.bfloat16, jnp.float32
    tile = (8, 128)
    slots = count + count // 2
    scratch = [
        pltpu.SMEM(cluster_of_block.shape, jnp.int32),
        vmem((rows // 128, 128), jnp.int32),
        vmem((rows // 128, 128), full),
        vmem((2 * count, rows, CHUNK), full),
        vmem((2 * count, rows, CHUNK), low),
        vmem((2, 2 * count, rows, CHUNK), low),
        vmem((NY - 1, count, rows, CHUNK), low),
        vmem((NY - 1, count, rows, CHUNK), low),
        vmem((NY - 1, rows, CHUNK), low),
        vmem((NY - 1, rows, CHUNK), low),
        vmem((2, count, rows, CHUNK), low),
        vmem((2, count, rows, CHUNK), low),
        vmem((2, slots, rows, CHUNK), low),
        vmem((2, slots, rows, CHUNK), low),
        vmem((rows, NY * rows), full),
        vmem((rows, NY * rows), full),
        vmem((NY, rows, rows), low),
        vmem((NY - 1, rows // 2, rows), low),
        vmem((NY - 1, rows // 2, rows), low),
        vmem((NY + 1, rows // 2, rows), low),
        vmem((NY + 1, rows // 2, rows), low),
        vmem((NY + 1, rows // 2, rows), low),
        vmem((NY, rows, rows), low),
        vmem((NY, rows, rows), low),
        vmem((rows, 128), full),
        vmem((rows, 128), full),
        vmem(tile, full),
        vmem((NY,) + tile, full),
        vmem((NZ,) + tile, full),
        vmem((NX,) + tile, full),
        dma((2 * count,)),
        dma((2, 2 * count)),
        dma((2, 2 * count)),
        dma((NY - 1, count)),
        dma((NY - 1, count)),
        dma, dma,
        dma((NY - 1,)), dma((NY - 1,)),
        dma((NY - 1,)), dma((NY - 1,)),
        dma, dma,
        dma((NY,)), dma((NY,)),
        dma((NZ,)), dma((NZ,)),
        dma((NX,)), dma((NX,)),
        dma((NY - 1,)), dma((NY - 1,)),
        dma((3,)),
        dma((2, slots)), dma((2, slots)),
        dma((2, count)), dma((2, count)),
    ]
    in_vmem = pl.BlockSpec(memory_space=pltpu.VMEM)
    loss, query_grad, passage_grad = pl.pallas_call(
        kernel,
        out_shape=[
            jax.ShapeDtypeStruct(tile, full),
            vmem((rows, width), full),
            vmem((rows, width), full),
        ],
        in_specs=[pl.BlockSpec(memory_space=pltpu.HBM)] * 5,
        out_specs=[in_vmem, in_vmem, in_vmem],
        scratch_shapes=scratch,
        compiler_params=pltpu.CompilerParams(
            collective_id=0, has_side_effects=True, vmem_limit_bytes=48 * 2**20
        ),
        cost_estimate=pl.CostEstimate(
            flops=6 * NY * rows * rows * width, bytes_accessed=16 * rows * width, transcendentals=NY * rows * rows
        ),
    )(
        *[
            pltpu.with_memory_space_constraint(array, pltpu.HBM)
            for array in (
                queries, passages, cluster_of_block,
                positive_row.reshape(rows // 128, 128), query_weight.reshape(rows // 128, 128),
            )
        ]
    )
    return loss[0, 0], query_grad, passage_grad


def solution(mesh):
    in_specs = (P("dp", "mp"), P("dp", "mp"), P(), P("dp"), P("dp"))
    out_specs = (P(), P("dp", "mp"), P("dp", "mp"))
    return jax.shard_map(shards, mesh=mesh, in_specs=in_specs, out_specs=out_specs, check_vma=False)
```

```python
import functools
import math

import jax
import jax.numpy as jnp
from jax import lax
from jax.experimental import pallas as pl
from jax.experimental.pallas import tpu as pltpu
from jax.sharding import PartitionSpec as P

MESH = pl.DeviceIdType.MESH
NY, NZ, NX = 4, 8, 4
CHUNK = 256
GROUP = 32
EASY = 1


def nt_dot(left, right):
    return lax.dot_general(left, right, (((1,), (1,)), ((), ())), preferred_element_type=jnp.float32)


def nn_dot(left, right):
    return jnp.dot(left, right, preferred_element_type=jnp.float32)


def kernel(
    query_hbm, passage_hbm, cluster_hbm, positive_hbm, weight_hbm,
    loss_ref, query_grad, passage_grad,
    cluster, positive, weight, fresh, own, beside, staged, gathered, raw, raw_beside,
    passed, across, ring_out, ring_in, late_in,
    score_own, score_other, coeff, coeff_out, coeff_beside, coeff_staged, coeff_got, coeff_fwd, coeff_t, middle_t,
    pos_cols, weight_cols, loss_tile, loss_core, loss_y, loss_z, loss_x,
    in_sem, z_send, z_recv, y_send, y_recv, s_send, s_recv,
    cz_send, cz_recv, cy_send, cy_recv, cf_send, cf_recv,
    ly_send, ly_recv, lz_send, lz_recv, lx_send, lx_recv, raw_send, raw_recv, small_sem, ring_send, ring_recv, hop_send, hop_recv,
    late_send, late_recv, ch_send, ch_recv, lc_send, lc_recv,
):
    rows, width = query_hbm.shape
    count = width // CHUNK
    half = rows // 2
    planes = NX * NZ
    me = lax.axis_index("dp")
    core = lax.axis_index("mp")
    y = me % NY
    plane = me // NY
    z = plane % NZ
    x = plane // NZ

    def at_y(step):
        return plane * NY + (y + step) % NY

    def at_z(step):
        return (x * NZ + (z + step) % NZ) * NY + y

    def at_x(step):
        return (((x + step) % NX) * NZ + z) * NY + y

    left_plane = ((plane + planes - 1) % planes) * NY + y
    right_plane = ((plane + 1) % planes) * NY + y
    one_way = [jnp.where(y + s < NY, right_plane, left_plane) for s in range(1, NY)]
    other_way = [jnp.where(y + s < NY, left_plane, right_plane) for s in range(1, NY)]

    def arriving(k):
        start = pl.multiple_of(k * CHUNK, CHUNK)
        return pltpu.make_async_copy(passage_hbm.at[:, pl.ds(start, CHUNK)], fresh.at[k], in_sem.at[k])

    def arriving_query(k):
        start = pl.multiple_of(k * CHUNK, CHUNK)
        return pltpu.make_async_copy(
            query_hbm.at[:, pl.ds(start, CHUNK)], fresh.at[count + k], in_sem.at[count + k]
        )

    def start_in(k, carry):
        arriving(k).start()
        return carry

    def start_in_query(k, carry):
        arriving_query(k).start()
        return carry

    small = [
        pltpu.make_async_copy(source, target, small_sem.at[i])
        for i, (source, target) in enumerate(
            [(cluster_hbm, cluster), (positive_hbm, positive), (weight_hbm, weight)]
        )
    ]
    arriving(0).start()
    for copy in small:
        copy.start()
    lax.fori_loop(1, count, start_in, 0)
    lax.fori_loop(0, count, start_in_query, 0)

    barrier = pltpu.get_barrier_semaphore()
    peers = [at_y(s) for s in range(1, NY)] + [at_z(s) for s in range(1, NZ)] + [at_x(s) for s in range(1, NX)]
    peers = peers + [left_plane, right_plane]
    for peer in peers:
        pl.semaphore_signal(barrier, inc=1, device_id=(peer, core), device_id_type=MESH)
    pl.semaphore_signal(barrier, inc=1, device_id=(me, 1 - core), device_id_type=MESH)
    pl.semaphore_wait(barrier, len(peers) + 1)

    for copy in small:
        copy.wait()

    last = planes * NY - 1
    mine = cluster[me]
    on_left = cluster[jnp.maximum(me - NY, 0)]
    on_right = cluster[jnp.minimum(me + NY, last)]
    has_left = plane > 0
    has_right = plane < planes - 1
    want_left, want_right, linked = [], [], [None]
    got_beside = [None]
    for step in range(1, NY):
        target = at_y(step)
        theirs = cluster[target]
        want_left.append(has_left & (theirs == on_left))
        want_right.append(has_right & (theirs == on_right))
        from_here = theirs == mine
        from_left = has_left & (cluster[jnp.maximum(target - NY, 0)] == mine)
        from_right = has_right & (cluster[jnp.minimum(target + NY, last)] == mine)
        linked.append(from_here | from_left | from_right)
        got_beside.append(from_left | from_right)

    def same(step):
        there = me + step
        inside = (there >= 0) & (there <= last)
        return inside & (cluster[jnp.clip(there, 0, last)] == mine)

    near_up, near_down = same(1), same(-1)
    far_up, far_down = same(2), same(-2)
    middle = near_up & near_down & jnp.logical_not(far_up) & jnp.logical_not(far_down)
    top_end = near_down & far_down & jnp.logical_not(same(-3)) & jnp.logical_not(near_up)
    low_end = near_up & far_up & jnp.logical_not(same(3)) & jnp.logical_not(near_down)
    from_beside = [want_left[0] | want_right[0], want_left[2] | want_right[2]]

    def pick(step, here, from_left, from_right):
        return lax.select(
            want_left[step - 1], from_left, lax.select(want_right[step - 1], from_right, here)
        )

    def send(source, target, send_sem, recv_sem, place, where=None):
        return pltpu.make_async_remote_copy(
            src_ref=source, dst_ref=target, send_sem=send_sem, recv_sem=recv_sem,
            device_id=(place, core if where is None else where), device_id_type=MESH,
        )

    def along_z(k):
        return [
            send(own.at[k], beside.at[0, k], z_send.at[0, k], z_recv.at[0, k], right_plane),
            send(own.at[k], beside.at[1, k], z_send.at[1, k], z_recv.at[1, k], left_plane),
        ]

    def along_y(k):
        return [
            send(
                staged.at[s - 1, k], gathered.at[NY - s - 1, k],
                y_send.at[s - 1, k], y_recv.at[NY - s - 1, k], at_y(s),
            )
            for s in range(1, NY)
        ]

    def share(k):
        for copy in along_z(k):
            copy.start()

    def relay(k):
        for copy in along_z(k):
            copy.wait_recv()
        here, from_left, from_right = own[k], beside[0, k], beside[1, k]
        for s in range(1, NY):
            staged[s - 1, k] = pick(s, here, from_left, from_right)
        for copy in along_y(k):
            copy.start()

    def landed(k):
        for copy in along_y(k):
            copy.wait_recv()

    def block(k, slot):
        return own[k] if slot == 0 else gathered[slot - 1, k]

    def add_scores(k, first=False):
        mine_now = own[count + k]
        for slot in range(NY):
            columns = slice(slot * rows, (slot + 1) * rows)
            part = nt_dot(mine_now, block(k, slot))
            if first:
                score_own[:, columns] = part
            else:
                score_own[:, columns] += part

    def cast_passage(k):
        arriving(k).wait()
        own[k] = fresh[k].astype(jnp.bfloat16)

    def first_along_y():
        return [
            send(own.at[0], raw.at[NY - s - 1], y_send.at[s - 1, 0], y_recv.at[NY - s - 1, 0], at_y(s))
            for s in range(1, NY)
        ]

    def first_along_z():
        return [
            send(raw.at[s - 1], raw_beside.at[s - 1], raw_send.at[s - 1], raw_recv.at[s - 1], one_way[s - 1])
            for s in range(1, NY)
        ]

    cast_passage(0)
    for copy in first_along_y():
        copy.start()
    for k in range(1, 4):
        cast_passage(k)
        share(k)

    def cast_rest(k, carry):
        cast_passage(k)
        return carry

    def cast_queries(k, carry):
        arriving_query(k).wait()
        own[count + k] = fresh[count + k].astype(jnp.bfloat16)
        return carry

    lax.fori_loop(4, count, cast_rest, 0)
    lax.fori_loop(0, count, cast_queries, 0)

    for part in range(rows // 128):
        here = slice(part * 128, (part + 1) * 128)
        as_row = positive[part : part + 1, :].astype(jnp.float32)
        pos_cols[here, :] = jnp.broadcast_to(as_row, (128, 128)).T
        weight_cols[here, :] = jnp.broadcast_to(weight[part : part + 1, :], (128, 128)).T

    relay(1)
    share(4)
    for copy in first_along_y():
        copy.wait_recv()
    relay(2)
    share(5)
    landed(1)
    add_scores(1, first=True)

    part = count // 2
    hop_place = [
        jnp.where(y == NY - 1, right_plane, left_plane),
        jnp.where(y == 0, left_plane, right_plane),
    ]
    wraps = [y == NY - 1, y == 0]
    steps = [1, NY - 1]

    def ring(way, q):
        return send(
            ring_out.at[way, q], ring_in.at[way, q], ring_send.at[way, q], ring_recv.at[way, q], at_y(steps[way])
        )

    def hop(way, j, relayed=False):
        source = ring_in.at[way, j] if relayed else passed.at[way, j]
        return send(source, across.at[way, j], hop_send.at[way, j], hop_recv.at[way, j], hop_place[way])

    late_place = [right_plane, left_plane]
    late_columns = [y == 0, y == NY - 1]
    late_wanted = [near_down, near_up]

    def late(way, j):
        return send(
            ring_in.at[way, part + j], late_in.at[way, j], late_send.at[way, j], late_recv.at[way, j], late_place[way]
        )

    def query_chunk(way, q):
        return count + (q + part) % count if way == 0 else count + q

    def ring_first(q):
        for k in (q, q + part):
            for copy in along_z(count + k):
                copy.wait_recv()
        for way in range(2):
            k = query_chunk(way, q)
            ring_out[way, q] = pick(steps[way], own[k], beside[0, k], beside[1, k])
            ring(way, q).start()

    def ring_landed(q):
        for way in range(2):
            ring(way, q).wait_recv()

    def pass_relayed(j):
        for way in range(2):

            @pl.when(jnp.logical_not(wraps[way]))
            def _():
                hop(way, j, True).start()

    def ring_second(j):
        q = part + j
        for way in range(2):
            k = query_chunk(way, q)
            here = lax.select(middle, ring_in[way, j], own[k])
            s = steps[way] - 1
            inside = jnp.logical_not(wraps[way])
            here = lax.select(inside & want_right[s], beside[1, k], here)
            ring_out[way, q] = lax.select(inside & want_left[s], beside[0, k], here)
            ring(way, q).start()

    def last_content(way, j):
        k = query_chunk(way, part + j)
        terms = nn_dot(middle_t[way], own[k]) + nn_dot(middle_t[2 + way], ring_in[way, part + j])
        passed[way, j] = lax.select(middle, terms.astype(jnp.bfloat16), ring_in[way, j])

    def start_late(j):
        for way in range(2):

            @pl.when(late_columns[way])
            def _():
                late(way, j).start()

    def finish_late(j):
        for way in range(2):

            @pl.when(late_columns[way])
            def _():
                late(way, j).wait()
                ring_in[way, part + j] = lax.select(late_wanted[way], late_in[way, j], ring_in[way, part + j])

    def begin_last(j):
        for way in range(2):

            @pl.when(wraps[way])
            def _():
                last_content(way, j)
                if j >= EASY:
                    hop(way, j).start()

    def finish_last(j):
        finish_late(j)
        for way in range(2):

            @pl.when(jnp.logical_not(wraps[way]))
            def _():
                last_content(way, j)

    def ring_last(j):
        q = count + j
        for way in range(2):
            if j >= EASY:
                hop(way, j).wait_recv()
                ring_out[way, q] = lax.select(from_beside[way], across[way, j], passed[way, j])
            else:

                @pl.when(wraps[way])
                def _():
                    ring_out[way, q] = passed[way, j]

                @pl.when(jnp.logical_not(wraps[way]))
                def _():
                    hop(way, j).wait_recv()
                    ring_out[way, q] = lax.select(from_beside[way], across[way, j], passed[way, j])

            ring(way, q).start()

    def passage_step(k, shares):
        relay(k)
        for share_now in shares:
            share(share_now)
        landed(k - 1)
        add_scores(k - 1)

    passage_step(3, [6])
    for copy in first_along_z():
        copy.start()
    passage_step(4, [7])
    for k in range(5, count):
        passage_step(k, [count + k - 5, count + part + k - 5])
    for copy in first_along_z():
        copy.wait_recv()
    for slot in range(1, NY):
        gathered[slot - 1, 0] = lax.select(got_beside[slot], raw_beside[slot - 1], raw[slot - 1])
    add_scores(0)
    share(count + part - 1)
    share(2 * count - 1)
    ring_first(0)
    landed(count - 1)
    ring_first(1)
    add_scores(count - 1)
    my_half = pl.ds(pl.multiple_of(core * half, half), half)
    their_half = pl.ds(pl.multiple_of((1 - core) * half, half), half)
    swap = send(score_own.at[their_half], score_other, s_send, s_recv, me, 1 - core)
    swap.start()
    ring_first(2)
    swap.wait_recv()

    scale = 3.0 / math.sqrt(2 * width)

    def soft_rows(group, total):
        here = pl.ds(pl.multiple_of(core * half + group * GROUP, GROUP), GROUP)
        there = pl.ds(pl.multiple_of(group * GROUP, GROUP), GROUP)
        tiles = []
        for slot in range(NY):
            columns = slice(slot * rows, (slot + 1) * rows)
            tile = (score_own[here, columns] + score_other[there, columns]) * scale
            if slot > 0:
                tile = lax.select(linked[slot], tile, jnp.full_like(tile, -1e30))
            tiles.append(tile)
        top = functools.reduce(jnp.maximum, [jnp.max(t, axis=1, keepdims=True) for t in tiles])
        expo = [jnp.exp(t - top) for t in tiles]
        row_total = functools.reduce(jnp.add, [jnp.sum(e, axis=1, keepdims=True) for e in expo])
        wanted = pos_cols[here, 0:1]
        heavy = weight_cols[here, 0:1]
        columns = lax.broadcasted_iota(jnp.int32, (GROUP, rows), 1).astype(jnp.float32)
        hit = columns == wanted
        picked = jnp.sum(jnp.where(hit, tiles[0], 0.0), axis=1, keepdims=True)
        ratio = heavy / row_total
        for slot in range(NY):
            value = expo[slot] * ratio
            if slot == 0:
                value = value - jnp.where(hit, heavy, 0.0)
            coeff[slot, here, :] = value.astype(jnp.bfloat16)
        return total + heavy * (top + jnp.log(row_total) - picked)

    total = lax.fori_loop(0, half // GROUP, soft_rows, jnp.zeros((GROUP, 1), jnp.float32))
    for s in range(1, NY):
        coeff_out[s - 1] = coeff[s, my_half, :]
    coeff_z = [
        send(coeff_out.at[s - 1], coeff_beside.at[s - 1], cz_send.at[s - 1], cz_recv.at[s - 1], other_way[s - 1])
        for s in range(1, NY)
    ]
    for copy in coeff_z:
        copy.start()

    halves = send(coeff.at[:, my_half, :], coeff.at[:, my_half, :], ch_send, ch_recv, me, 1 - core)
    halves.start()
    loss_core[core] = jnp.broadcast_to(jnp.sum(total, axis=0, keepdims=True), loss_tile.shape)
    loss_across = send(loss_core.at[core], loss_core.at[core], lc_send, lc_recv.at[core], me, 1 - core)
    loss_across.start()

    def spread(buffer, send_sem, recv_sem, mine_at, size, place):
        return [
            send(loss_tile, buffer.at[mine_at], send_sem.at[s - 1], recv_sem.at[mine_at], place(s))
            for s in range(1, size)
        ]

    def collect(buffer, recv_sem, mine_at, size):
        buffer[mine_at] = loss_tile[...]
        for s in range(1, size):
            source = (mine_at + s) % size
            send(loss_tile, buffer.at[source], recv_sem.at[source], recv_sem.at[source], me, 1 - core).wait_recv()
        value = buffer[0]
        for s in range(1, size):
            value = value + buffer[s]
        return value

    ring_first(3)
    ring_landed(0)
    ring_landed(1)
    halves.wait_recv()

    def query_grad_step(k, carry):
        value = nn_dot(coeff[0], own[k])
        for slot in range(1, NY):
            value = value + nn_dot(coeff[slot], gathered[slot - 1, k])
        query_grad[:, pl.ds(pl.multiple_of(k * CHUNK, CHUNK), CHUNK)] = value
        return carry

    lax.fori_loop(0, count, query_grad_step, 0)

    send(
        loss_core.at[1 - core], loss_core.at[1 - core], lc_send, lc_recv.at[1 - core], me, 1 - core
    ).wait_recv()
    loss_tile[...] = loss_core[0] + loss_core[1]
    loss_along_y = spread(loss_y, ly_send, ly_recv, y, NY, at_y)
    for copy in loss_along_y:
        copy.start()

    for copy in coeff_z:
        copy.wait_recv()
    for place, (s, tile) in enumerate([(1, 1), (1, 2), (2, 2), (3, 3), (3, 2)]):
        coeff_staged[place] = lax.select(
            want_left[s - 1] | want_right[s - 1], coeff_beside[tile - 1], coeff_out[tile - 1]
        )
    coeff_y = [
        send(coeff_staged.at[0:2], coeff_got.at[3:5], cy_send.at[0], cy_recv.at[2], at_y(1)),
        send(coeff_staged.at[2], coeff_got.at[2], cy_send.at[1], cy_recv.at[1], at_y(2)),
        send(coeff_staged.at[3:5], coeff_got.at[0:2], cy_send.at[2], cy_recv.at[0], at_y(3)),
    ]
    for message in (0, 2, 1):
        coeff_y[message].start()

    ring_second(0)
    pass_relayed(0)
    pass_relayed(1)
    ring_landed(2)
    pass_relayed(2)
    ring_second(1)
    ring_landed(3)
    pass_relayed(3)
    value = collect(loss_y, ly_recv, y, NY)
    for copy in loss_along_y:
        copy.wait_send()
    loss_tile[...] = value
    loss_along_z = spread(loss_z, lz_send, lz_recv, z, NZ, at_z)
    for copy in loss_along_z:
        copy.start()
    ring_second(2)
    coeff_y[0].wait_recv()
    coeff_y[2].wait_recv()
    forward = [
        send(coeff_got.at[piece], coeff_fwd.at[piece], cf_send.at[i], cf_recv.at[i], me, 1 - core)
        for i, piece in enumerate((slice(0, 2), slice(2, 3), slice(3, 5)))
    ]
    forward[0].start()
    forward[2].start()
    ring_second(3)

    def turned(tile):
        return tile.astype(jnp.float32).T

    coeff_t[0] = turned(coeff[0]).astype(jnp.bfloat16)
    middle_t[0] = turned(coeff[1]).astype(jnp.bfloat16)
    middle_t[1] = turned(coeff[3]).astype(jnp.bfloat16)
    ring_landed(4)
    start_late(0)
    forward[0].wait_recv()
    forward[2].wait_recv()
    first_half = core == 0

    def whole(place):
        got, fwd = coeff_got[place], coeff_fwd[place]
        return turned(
            jnp.concatenate([lax.select(first_half, got, fwd), lax.select(first_half, fwd, got)], axis=0)
        )

    middle_t[2] = whole(4).astype(jnp.bfloat16)
    middle_t[3] = whole(1).astype(jnp.bfloat16)
    begin_last(0)
    coeff_y[1].wait_recv()
    forward[1].start()
    ring_landed(5)
    start_late(1)
    begin_last(1)
    finish_last(0)
    ring_last(0)
    forward[1].wait_recv()
    for slot, place in ((1, 0), (2, 2), (3, 3)):
        tile = whole(place)
        coeff_t[slot] = lax.select(linked[slot], tile, jnp.zeros_like(tile)).astype(jnp.bfloat16)
    ring_landed(6)
    start_late(2)
    begin_last(2)
    finish_last(1)
    ring_last(1)
    ring_landed(7)
    start_late(3)
    begin_last(3)
    finish_last(2)
    ring_last(2)
    value = collect(loss_z, lz_recv, z, NZ)
    for copy in loss_along_z:
        copy.wait_send()
    loss_tile[...] = value
    loss_along_x = spread(loss_x, lx_send, lx_recv, x, NX, at_x)
    for copy in loss_along_x:
        copy.start()
    finish_last(3)
    ring_last(3)

    def passage_grad_chunk(k, start):
        j = k % part
        up, down = ring_in[0, (k + part) % count], ring_in[1, k]
        far = ring_in[1 if start else 0, count + j]
        relayed = ring_in[1 if start else 0, part + j]
        near_end, far_end = (low_end, top_end) if start else (top_end, low_end)
        done = ring_in[0 if start else 1, count + j].astype(jnp.float32)
        from_up = nn_dot(coeff_t[NY - 1], up)
        from_down = nn_dot(coeff_t[1], down)
        if start:
            from_up = lax.select(far_end, done, from_up)
        else:
            from_down = lax.select(far_end, done, from_down)
        opposite = nn_dot(coeff_t[2], lax.select(near_end, relayed, far))
        opposite = lax.select(far_end, jnp.zeros_like(opposite), opposite)
        value = nn_dot(coeff_t[0], own[count + k]) + from_up + from_down + opposite
        passage_grad[:, k * CHUNK : (k + 1) * CHUNK] = value

    for j in range(EASY):
        ring_landed(count + j)
        start_late(part + j)
    value = collect(loss_x, lx_recv, x, NX)
    for copy in loss_along_x:
        copy.wait_send()
    loss_ref[...] = value * (1.0 / (rows * planes * NY))
    for j in range(EASY, part):
        ring_landed(count + j)
        if j == EASY:
            for i in range(EASY):
                finish_late(part + i)
                passage_grad_chunk(i, True)
                passage_grad_chunk(part + i, False)
        passage_grad_chunk(j, True)
        passage_grad_chunk(part + j, False)

    def finish_shares(k, carry):
        for copy in along_z(k):
            copy.wait_send()
        return carry

    def finish_chunks(k, carry):
        for copy in along_y(k):
            copy.wait_send()
        return carry

    def finish_ring(q, carry):
        for way in range(2):
            ring(way, q).wait_send()
        return carry

    def finish_hops(j, carry):
        for way in range(2):
            hop(way, j).wait_send()
        return carry

    lax.fori_loop(1, 2 * count, finish_shares, 0)
    lax.fori_loop(1, count, finish_chunks, 0)
    lax.fori_loop(0, count + part, finish_ring, 0)
    for way in range(2):

        @pl.when(jnp.logical_not(wraps[way]))
        def _():
            for j in range(EASY):
                hop(way, j).wait_send()

    lax.fori_loop(EASY, part, finish_hops, 0)
    for copy in first_along_y() + first_along_z() + coeff_z + coeff_y + forward + [swap, halves, loss_across]:
        copy.wait_send()


def shards(queries, passages, cluster_of_block, positive_row, query_weight):
    rows, width = queries.shape
    count = width // CHUNK
    dma = pltpu.SemaphoreType.DMA
    vmem = pltpu.VMEM
    low, full = jnp.bfloat16, jnp.float32
    tile = (8, 128)
    slots = count + count // 2
    scratch = [
        pltpu.SMEM(cluster_of_block.shape, jnp.int32),
        vmem((rows // 128, 128), jnp.int32),
        vmem((rows // 128, 128), full),
        vmem((2 * count, rows, CHUNK), full),
        vmem((2 * count, rows, CHUNK), low),
        vmem((2, 2 * count, rows, CHUNK), low),
        vmem((NY - 1, count, rows, CHUNK), low),
        vmem((NY - 1, count, rows, CHUNK), low),
        vmem((NY - 1, rows, CHUNK), low),
        vmem((NY - 1, rows, CHUNK), low),
        vmem((2, count // 2, rows, CHUNK), low),
        vmem((2, count // 2, rows, CHUNK), low),
        vmem((2, slots, rows, CHUNK), low),
        vmem((2, slots, rows, CHUNK), low),
        vmem((2, count // 2 + EASY, rows, CHUNK), low),
        vmem((rows, NY * rows), full),
        vmem((rows // 2, NY * rows), full),
        vmem((NY, rows, rows), low),
        vmem((NY - 1, rows // 2, rows), low),
        vmem((NY - 1, rows // 2, rows), low),
        vmem((NY + 1, rows // 2, rows), low),
        vmem((NY + 1, rows // 2, rows), low),
        vmem((NY + 1, rows // 2, rows), low),
        vmem((NY, rows, rows), low),
        vmem((NY, rows, rows), low),
        vmem((rows, 128), full),
        vmem((rows, 128), full),
        vmem(tile, full),
        vmem((2,) + tile, full),
        vmem((NY,) + tile, full),
        vmem((NZ,) + tile, full),
        vmem((NX,) + tile, full),
        dma((2 * count,)),
        dma((2, 2 * count)),
        dma((2, 2 * count)),
        dma((NY - 1, count)),
        dma((NY - 1, count)),
        dma, dma,
        dma((NY - 1,)), dma((NY - 1,)),
        dma((NY - 1,)), dma((NY - 1,)),
        dma((3,)), dma((3,)),
        dma((NY,)), dma((NY,)),
        dma((NZ,)), dma((NZ,)),
        dma((NX,)), dma((NX,)),
        dma((NY - 1,)), dma((NY - 1,)),
        dma((3,)),
        dma((2, slots)), dma((2, slots)),
        dma((2, count // 2)), dma((2, count // 2)),
        dma((2, count // 2 + EASY)), dma((2, count // 2 + EASY)),
        dma, dma,
        dma, dma((2,)),
    ]
    in_vmem = pl.BlockSpec(memory_space=pltpu.VMEM)
    loss, query_grad, passage_grad = pl.pallas_call(
        kernel,
        out_shape=[
            jax.ShapeDtypeStruct(tile, full),
            vmem((rows, width), full),
            vmem((rows, width), full),
        ],
        in_specs=[pl.BlockSpec(memory_space=pltpu.HBM)] * 5,
        out_specs=[in_vmem, in_vmem, in_vmem],
        scratch_shapes=scratch,
        compiler_params=pltpu.CompilerParams(
            collective_id=0, has_side_effects=True, vmem_limit_bytes=48 * 2**20
        ),
        cost_estimate=pl.CostEstimate(
            flops=6 * NY * rows * rows * width, bytes_accessed=16 * rows * width, transcendentals=NY * rows * rows
        ),
    )(
        *[
            pltpu.with_memory_space_constraint(array, pltpu.HBM)
            for array in (
                queries, passages, cluster_of_block,
                positive_row.reshape(rows // 128, 128), query_weight.reshape(rows // 128, 128),
            )
        ]
    )
    return loss[0, 0], query_grad, passage_grad


def solution(mesh):
    in_specs = (P("dp", "mp"), P("dp", "mp"), P(), P("dp"), P("dp"))
    out_specs = (P(), P("dp", "mp"), P("dp", "mp"))
    return jax.shard_map(shards, mesh=mesh, in_specs=in_specs, out_specs=out_specs, check_vma=False)
```

```python
import functools
import math

import jax
import jax.numpy as jnp
from jax import lax
from jax.experimental import pallas as pl
from jax.experimental.pallas import tpu as pltpu
from jax.sharding import PartitionSpec as P

MESH = pl.DeviceIdType.MESH
NY, NZ, NX = 4, 8, 4
CHUNK = 256
GROUP = 32
EASY = 1


def nt_dot(left, right):
    return lax.dot_general(left, right, (((1,), (1,)), ((), ())), preferred_element_type=jnp.float32)


def nn_dot(left, right):
    return jnp.dot(left, right, preferred_element_type=jnp.float32)


def kernel(
    query_hbm, passage_hbm, cluster_hbm, positive_hbm, weight_hbm,
    loss_ref, query_grad, passage_grad,
    cluster, positive, weight, fresh, own, beside, staged, gathered, raw, raw_beside,
    passed, across, ring_out, ring_in, late_in,
    score_own, score_other, coeff, coeff_out, coeff_beside, coeff_staged, coeff_got, coeff_fwd, coeff_t, middle_t,
    pos_cols, weight_cols, loss_tile, loss_core, loss_y, loss_z, loss_x,
    in_sem, z_send, z_recv, y_send, y_recv, s_send, s_recv,
    cz_send, cz_recv, cy_send, cy_recv, cf_send, cf_recv,
    ly_send, ly_recv, lz_send, lz_recv, lx_send, lx_recv, raw_send, raw_recv, small_sem, ring_send, ring_recv, hop_send, hop_recv,
    late_send, late_recv, ch_send, ch_recv, lc_send, lc_recv,
):
    rows, width = query_hbm.shape
    count = width // CHUNK
    half = rows // 2
    planes = NX * NZ
    me = lax.axis_index("dp")
    core = lax.axis_index("mp")
    y = me % NY
    plane = me // NY
    z = plane % NZ
    x = plane // NZ

    def at_y(step):
        return plane * NY + (y + step) % NY

    def at_z(step):
        return (x * NZ + (z + step) % NZ) * NY + y

    def at_x(step):
        return (((x + step) % NX) * NZ + z) * NY + y

    left_plane = ((plane + planes - 1) % planes) * NY + y
    right_plane = ((plane + 1) % planes) * NY + y
    one_way = [jnp.where(y + s < NY, right_plane, left_plane) for s in range(1, NY)]
    other_way = [jnp.where(y + s < NY, left_plane, right_plane) for s in range(1, NY)]

    def arriving(k):
        start = pl.multiple_of(k * CHUNK, CHUNK)
        return pltpu.make_async_copy(passage_hbm.at[:, pl.ds(start, CHUNK)], fresh.at[k], in_sem.at[k])

    def arriving_query(k):
        start = pl.multiple_of(k * CHUNK, CHUNK)
        return pltpu.make_async_copy(
            query_hbm.at[:, pl.ds(start, CHUNK)], fresh.at[count + k], in_sem.at[count + k]
        )

    def start_in(k, carry):
        arriving(k).start()
        return carry

    def start_in_query(k, carry):
        arriving_query(k).start()
        return carry

    small = [
        pltpu.make_async_copy(source, target, small_sem.at[i])
        for i, (source, target) in enumerate(
            [(cluster_hbm, cluster), (positive_hbm, positive), (weight_hbm, weight)]
        )
    ]
    arriving(0).start()
    for copy in small:
        copy.start()
    lax.fori_loop(1, count, start_in, 0)
    lax.fori_loop(0, count, start_in_query, 0)

    barrier = pltpu.get_barrier_semaphore()
    peers = [at_y(s) for s in range(1, NY)] + [at_z(s) for s in range(1, NZ)] + [at_x(s) for s in range(1, NX)]
    peers = peers + [left_plane, right_plane]
    for peer in peers:
        pl.semaphore_signal(barrier, inc=1, device_id=(peer, core), device_id_type=MESH)
    pl.semaphore_signal(barrier, inc=1, device_id=(me, 1 - core), device_id_type=MESH)
    for copy in small:
        copy.wait()

    last = planes * NY - 1
    mine = cluster[me]
    on_left = cluster[jnp.maximum(me - NY, 0)]
    on_right = cluster[jnp.minimum(me + NY, last)]
    has_left = plane > 0
    has_right = plane < planes - 1
    want_left, want_right, linked = [], [], [None]
    got_beside = [None]
    for step in range(1, NY):
        target = at_y(step)
        theirs = cluster[target]
        want_left.append(has_left & (theirs == on_left))
        want_right.append(has_right & (theirs == on_right))
        from_here = theirs == mine
        from_left = has_left & (cluster[jnp.maximum(target - NY, 0)] == mine)
        from_right = has_right & (cluster[jnp.minimum(target + NY, last)] == mine)
        linked.append(from_here | from_left | from_right)
        got_beside.append(from_left | from_right)

    def same(step):
        there = me + step
        inside = (there >= 0) & (there <= last)
        return inside & (cluster[jnp.clip(there, 0, last)] == mine)

    near_up, near_down = same(1), same(-1)
    far_up, far_down = same(2), same(-2)
    middle = near_up & near_down & jnp.logical_not(far_up) & jnp.logical_not(far_down)
    top_end = near_down & far_down & jnp.logical_not(same(-3)) & jnp.logical_not(near_up)
    low_end = near_up & far_up & jnp.logical_not(same(3)) & jnp.logical_not(near_down)
    from_beside = [want_left[0] | want_right[0], want_left[2] | want_right[2]]

    def pick(step, here, from_left, from_right):
        return lax.select(
            want_left[step - 1], from_left, lax.select(want_right[step - 1], from_right, here)
        )

    def send(source, target, send_sem, recv_sem, place, where=None):
        return pltpu.make_async_remote_copy(
            src_ref=source, dst_ref=target, send_sem=send_sem, recv_sem=recv_sem,
            device_id=(place, core if where is None else where), device_id_type=MESH,
        )

    def along_z(k):
        return [
            send(own.at[k], beside.at[0, k], z_send.at[0, k], z_recv.at[0, k], right_plane),
            send(own.at[k], beside.at[1, k], z_send.at[1, k], z_recv.at[1, k], left_plane),
        ]

    def along_y(k):
        return [
            send(
                staged.at[s - 1, k], gathered.at[NY - s - 1, k],
                y_send.at[s - 1, k], y_recv.at[NY - s - 1, k], at_y(s),
            )
            for s in range(1, NY)
        ]

    def share(k):
        for copy in along_z(k):
            copy.start()

    def relay(k):
        for copy in along_z(k):
            copy.wait_recv()
        here, from_left, from_right = own[k], beside[0, k], beside[1, k]
        for s in range(1, NY):
            staged[s - 1, k] = pick(s, here, from_left, from_right)
        for copy in along_y(k):
            copy.start()

    def landed(k):
        for copy in along_y(k):
            copy.wait_recv()

    def block(k, slot):
        return own[k] if slot == 0 else gathered[slot - 1, k]

    def add_scores(k, first=False):
        mine_now = own[count + k]
        for slot in range(NY):
            columns = slice(slot * rows, (slot + 1) * rows)
            part = nt_dot(mine_now, block(k, slot))
            if first:
                score_own[:, columns] = part
            else:
                score_own[:, columns] += part

    def cast_passage(k):
        arriving(k).wait()
        own[k] = fresh[k].astype(jnp.bfloat16)

    def first_along_y():
        return [
            send(own.at[0], raw.at[NY - s - 1], y_send.at[s - 1, 0], y_recv.at[NY - s - 1, 0], at_y(s))
            for s in range(1, NY)
        ]

    def first_along_z():
        return [
            send(raw.at[s - 1], raw_beside.at[s - 1], raw_send.at[s - 1], raw_recv.at[s - 1], one_way[s - 1])
            for s in range(1, NY)
        ]

    cast_passage(0)
    pl.semaphore_wait(barrier, len(peers) + 1)
    for copy in first_along_y():
        copy.start()
    for k in range(1, 4):
        cast_passage(k)
        share(k)

    def cast_rest(k, carry):
        cast_passage(k)
        return carry

    def cast_queries(k, carry):
        arriving_query(k).wait()
        own[count + k] = fresh[count + k].astype(jnp.bfloat16)
        return carry

    lax.fori_loop(4, count, cast_rest, 0)
    lax.fori_loop(0, count, cast_queries, 0)

    for part in range(rows // 128):
        here = slice(part * 128, (part + 1) * 128)
        as_row = positive[part : part + 1, :].astype(jnp.float32)
        pos_cols[here, :] = jnp.broadcast_to(as_row, (128, 128)).T
        weight_cols[here, :] = jnp.broadcast_to(weight[part : part + 1, :], (128, 128)).T

    relay(1)
    share(4)
    for copy in first_along_y():
        copy.wait_recv()
    relay(2)
    share(5)
    landed(1)
    add_scores(1, first=True)

    part = count // 2
    hop_place = [
        jnp.where(y == NY - 1, right_plane, left_plane),
        jnp.where(y == 0, left_plane, right_plane),
    ]
    wraps = [y == NY - 1, y == 0]
    steps = [1, NY - 1]

    def ring(way, q):
        return send(
            ring_out.at[way, q], ring_in.at[way, q], ring_send.at[way, q], ring_recv.at[way, q], at_y(steps[way])
        )

    def hop(way, j, relayed=False):
        source = ring_in.at[way, j] if relayed else passed.at[way, j]
        return send(source, across.at[way, j], hop_send.at[way, j], hop_recv.at[way, j], hop_place[way])

    late_place = [right_plane, left_plane]
    late_columns = [y == 0, y == NY - 1]
    late_wanted = [near_down, near_up]

    def late(way, j):
        return send(
            ring_in.at[way, part + j], late_in.at[way, j], late_send.at[way, j], late_recv.at[way, j], late_place[way]
        )

    def query_chunk(way, q):
        return count + (q + part) % count if way == 0 else count + q

    def ring_first(q):
        for k in (q, q + part):
            for copy in along_z(count + k):
                copy.wait_recv()
        for way in range(2):
            k = query_chunk(way, q)
            ring_out[way, q] = pick(steps[way], own[k], beside[0, k], beside[1, k])
            ring(way, q).start()

    def ring_landed(q):
        for way in range(2):
            ring(way, q).wait_recv()

    def pass_relayed(j):
        for way in range(2):

            @pl.when(jnp.logical_not(wraps[way]))
            def _():
                hop(way, j, True).start()

    def ring_second(j):
        q = part + j
        for way in range(2):
            k = query_chunk(way, q)
            here = lax.select(middle, ring_in[way, j], own[k])
            s = steps[way] - 1
            inside = jnp.logical_not(wraps[way])
            here = lax.select(inside & want_right[s], beside[1, k], here)
            ring_out[way, q] = lax.select(inside & want_left[s], beside[0, k], here)
            ring(way, q).start()

    def last_content(way, j):
        k = query_chunk(way, part + j)
        terms = nn_dot(middle_t[way], own[k]) + nn_dot(middle_t[2 + way], ring_in[way, part + j])
        passed[way, j] = lax.select(middle, terms.astype(jnp.bfloat16), ring_in[way, j])

    def start_late(j):
        for way in range(2):

            @pl.when(late_columns[way])
            def _():
                late(way, j).start()

    def finish_late(j):
        for way in range(2):

            @pl.when(late_columns[way])
            def _():
                late(way, j).wait()
                ring_in[way, part + j] = lax.select(late_wanted[way], late_in[way, j], ring_in[way, part + j])

    def begin_last(j):
        for way in range(2):

            @pl.when(wraps[way])
            def _():
                last_content(way, j)
                if j >= EASY:
                    hop(way, j).start()

    def finish_last(j):
        finish_late(j)
        for way in range(2):

            @pl.when(jnp.logical_not(wraps[way]))
            def _():
                last_content(way, j)

    def ring_last(j):
        q = count + j
        for way in range(2):
            if j >= EASY:
                hop(way, j).wait_recv()
                ring_out[way, q] = lax.select(from_beside[way], across[way, j], passed[way, j])
            else:

                @pl.when(wraps[way])
                def _():
                    ring_out[way, q] = passed[way, j]

                @pl.when(jnp.logical_not(wraps[way]))
                def _():
                    hop(way, j).wait_recv()
                    ring_out[way, q] = lax.select(from_beside[way], across[way, j], passed[way, j])

            ring(way, q).start()

    def passage_step(k, shares):
        relay(k)
        for share_now in shares:
            share(share_now)
        landed(k - 1)
        add_scores(k - 1)

    passage_step(3, [6])
    for copy in first_along_z():
        copy.start()
    passage_step(4, [7])
    for k in range(5, count):
        passage_step(k, [count + k - 5, count + part + k - 5])
    for copy in first_along_z():
        copy.wait_recv()
    for slot in range(1, NY):
        gathered[slot - 1, 0] = lax.select(got_beside[slot], raw_beside[slot - 1], raw[slot - 1])
    add_scores(0)
    share(count + part - 1)
    share(2 * count - 1)
    ring_first(0)
    landed(count - 1)
    ring_first(1)
    add_scores(count - 1)
    my_half = pl.ds(pl.multiple_of(core * half, half), half)
    their_half = pl.ds(pl.multiple_of((1 - core) * half, half), half)
    swap = send(score_own.at[their_half], score_other, s_send, s_recv, me, 1 - core)
    swap.start()
    ring_first(2)
    swap.wait_recv()

    scale = 3.0 / math.sqrt(2 * width)

    def soft_rows(group, total):
        here = pl.ds(pl.multiple_of(core * half + group * GROUP, GROUP), GROUP)
        there = pl.ds(pl.multiple_of(group * GROUP, GROUP), GROUP)
        tiles = []
        for slot in range(NY):
            columns = slice(slot * rows, (slot + 1) * rows)
            tile = (score_own[here, columns] + score_other[there, columns]) * scale
            if slot > 0:
                tile = lax.select(linked[slot], tile, jnp.full_like(tile, -1e30))
            tiles.append(tile)
        top = functools.reduce(jnp.maximum, [jnp.max(t, axis=1, keepdims=True) for t in tiles])
        expo = [jnp.exp(t - top) for t in tiles]
        row_total = functools.reduce(jnp.add, [jnp.sum(e, axis=1, keepdims=True) for e in expo])
        wanted = pos_cols[here, 0:1]
        heavy = weight_cols[here, 0:1]
        columns = lax.broadcasted_iota(jnp.int32, (GROUP, rows), 1).astype(jnp.float32)
        hit = columns == wanted
        picked = jnp.sum(jnp.where(hit, tiles[0], 0.0), axis=1, keepdims=True)
        ratio = heavy / row_total
        for slot in range(NY):
            value = expo[slot] * ratio
            if slot == 0:
                value = value - jnp.where(hit, heavy, 0.0)
            coeff[slot, here, :] = value.astype(jnp.bfloat16)
        return total + heavy * (top + jnp.log(row_total) - picked)

    total = lax.fori_loop(0, half // GROUP, soft_rows, jnp.zeros((GROUP, 1), jnp.float32))
    for s in range(1, NY):
        coeff_out[s - 1] = coeff[s, my_half, :]
    coeff_z = [
        send(coeff_out.at[s - 1], coeff_beside.at[s - 1], cz_send.at[s - 1], cz_recv.at[s - 1], other_way[s - 1])
        for s in range(1, NY)
    ]
    for copy in coeff_z:
        copy.start()

    halves = send(coeff.at[:, my_half, :], coeff.at[:, my_half, :], ch_send, ch_recv, me, 1 - core)
    halves.start()
    loss_core[core] = jnp.broadcast_to(jnp.sum(total, axis=0, keepdims=True), loss_tile.shape)
    loss_across = send(loss_core.at[core], loss_core.at[core], lc_send, lc_recv.at[core], me, 1 - core)
    loss_across.start()

    def spread(buffer, send_sem, recv_sem, mine_at, size, place):
        return [
            send(loss_tile, buffer.at[mine_at], send_sem.at[s - 1], recv_sem.at[mine_at], place(s))
            for s in range(1, size)
        ]

    def collect(buffer, recv_sem, mine_at, size):
        buffer[mine_at] = loss_tile[...]
        for s in range(1, size):
            source = (mine_at + s) % size
            send(loss_tile, buffer.at[source], recv_sem.at[source], recv_sem.at[source], me, 1 - core).wait_recv()
        value = buffer[0]
        for s in range(1, size):
            value = value + buffer[s]
        return value

    ring_first(3)
    ring_landed(0)
    ring_landed(1)
    halves.wait_recv()

    def query_grad_step(k, carry):
        value = nn_dot(coeff[0], own[k])
        for slot in range(1, NY):
            value = value + nn_dot(coeff[slot], gathered[slot - 1, k])
        query_grad[:, pl.ds(pl.multiple_of(k * CHUNK, CHUNK), CHUNK)] = value
        return carry

    lax.fori_loop(0, count, query_grad_step, 0)

    send(
        loss_core.at[1 - core], loss_core.at[1 - core], lc_send, lc_recv.at[1 - core], me, 1 - core
    ).wait_recv()
    loss_tile[...] = loss_core[0] + loss_core[1]
    loss_along_y = spread(loss_y, ly_send, ly_recv, y, NY, at_y)
    for copy in loss_along_y:
        copy.start()

    for copy in coeff_z:
        copy.wait_recv()
    for place, (s, tile) in enumerate([(1, 1), (1, 2), (2, 2), (3, 3), (3, 2)]):
        coeff_staged[place] = lax.select(
            want_left[s - 1] | want_right[s - 1], coeff_beside[tile - 1], coeff_out[tile - 1]
        )
    coeff_y = [
        send(coeff_staged.at[0:2], coeff_got.at[3:5], cy_send.at[0], cy_recv.at[2], at_y(1)),
        send(coeff_staged.at[2], coeff_got.at[2], cy_send.at[1], cy_recv.at[1], at_y(2)),
        send(coeff_staged.at[3:5], coeff_got.at[0:2], cy_send.at[2], cy_recv.at[0], at_y(3)),
    ]
    for message in (0, 2, 1):
        coeff_y[message].start()

    ring_second(0)
    pass_relayed(0)
    pass_relayed(1)
    ring_landed(2)
    pass_relayed(2)
    ring_second(1)
    ring_landed(3)
    pass_relayed(3)
    value = collect(loss_y, ly_recv, y, NY)
    for copy in loss_along_y:
        copy.wait_send()
    loss_tile[...] = value
    loss_along_z = spread(loss_z, lz_send, lz_recv, z, NZ, at_z)
    for copy in loss_along_z:
        copy.start()
    ring_second(2)
    coeff_y[0].wait_recv()
    coeff_y[2].wait_recv()
    forward = [
        send(coeff_got.at[piece], coeff_fwd.at[piece], cf_send.at[i], cf_recv.at[i], me, 1 - core)
        for i, piece in enumerate((slice(0, 2), slice(2, 3), slice(3, 5)))
    ]
    forward[0].start()
    forward[2].start()
    ring_second(3)

    def turned(tile):
        return tile.astype(jnp.float32).T

    coeff_t[0] = turned(coeff[0]).astype(jnp.bfloat16)
    middle_t[0] = turned(coeff[1]).astype(jnp.bfloat16)
    middle_t[1] = turned(coeff[3]).astype(jnp.bfloat16)
    ring_landed(4)
    start_late(0)
    forward[0].wait_recv()
    forward[2].wait_recv()
    first_half = core == 0

    def whole(place):
        got, fwd = coeff_got[place], coeff_fwd[place]
        return turned(
            jnp.concatenate([lax.select(first_half, got, fwd), lax.select(first_half, fwd, got)], axis=0)
        )

    middle_t[2] = whole(4).astype(jnp.bfloat16)
    middle_t[3] = whole(1).astype(jnp.bfloat16)
    begin_last(0)
    coeff_y[1].wait_recv()
    forward[1].start()
    ring_landed(5)
    start_late(1)
    begin_last(1)
    finish_last(0)
    ring_last(0)
    forward[1].wait_recv()
    for slot, place in ((1, 0), (2, 2), (3, 3)):
        tile = whole(place)
        coeff_t[slot] = lax.select(linked[slot], tile, jnp.zeros_like(tile)).astype(jnp.bfloat16)
    ring_landed(6)
    start_late(2)
    begin_last(2)
    finish_last(1)
    ring_last(1)
    ring_landed(7)
    start_late(3)
    begin_last(3)
    finish_last(2)
    ring_last(2)
    value = collect(loss_z, lz_recv, z, NZ)
    for copy in loss_along_z:
        copy.wait_send()
    loss_tile[...] = value
    loss_along_x = spread(loss_x, lx_send, lx_recv, x, NX, at_x)
    for copy in loss_along_x:
        copy.start()
    finish_last(3)
    ring_last(3)

    def passage_grad_chunk(k, start):
        j = k % part
        up, down = ring_in[0, (k + part) % count], ring_in[1, k]
        far = ring_in[1 if start else 0, count + j]
        relayed = ring_in[1 if start else 0, part + j]
        near_end, far_end = (low_end, top_end) if start else (top_end, low_end)
        done = ring_in[0 if start else 1, count + j].astype(jnp.float32)
        from_up = nn_dot(coeff_t[NY - 1], up)
        from_down = nn_dot(coeff_t[1], down)
        if start:
            from_up = lax.select(far_end, done, from_up)
        else:
            from_down = lax.select(far_end, done, from_down)
        opposite = nn_dot(coeff_t[2], lax.select(near_end, relayed, far))
        opposite = lax.select(far_end, jnp.zeros_like(opposite), opposite)
        value = nn_dot(coeff_t[0], own[count + k]) + from_up + from_down + opposite
        passage_grad[:, k * CHUNK : (k + 1) * CHUNK] = value

    for j in range(EASY):
        ring_landed(count + j)
        start_late(part + j)
    value = collect(loss_x, lx_recv, x, NX)
    for copy in loss_along_x:
        copy.wait_send()
    loss_ref[...] = value * (1.0 / (rows * planes * NY))
    for j in range(EASY, part - 1):
        ring_landed(count + j)
        if j == EASY:
            for i in range(EASY):
                finish_late(part + i)
                passage_grad_chunk(i, True)
                passage_grad_chunk(part + i, False)
        passage_grad_chunk(j, True)
        passage_grad_chunk(part + j, False)

    def finish_shares(k, carry):
        for copy in along_z(k):
            copy.wait_send()
        return carry

    def finish_chunks(k, carry):
        for copy in along_y(k):
            copy.wait_send()
        return carry

    def finish_ring(q, carry):
        for way in range(2):
            ring(way, q).wait_send()
        return carry

    def finish_hops(j, carry):
        for way in range(2):
            hop(way, j).wait_send()
        return carry

    lax.fori_loop(1, 2 * count, finish_shares, 0)
    lax.fori_loop(1, count, finish_chunks, 0)
    lax.fori_loop(0, count + part - 2, finish_ring, 0)
    for way in range(2):

        @pl.when(jnp.logical_not(wraps[way]))
        def _():
            for j in range(EASY):
                hop(way, j).wait_send()

    lax.fori_loop(EASY, part, finish_hops, 0)
    for copy in first_along_y() + first_along_z() + coeff_z + coeff_y + forward + [swap, halves, loss_across]:
        copy.wait_send()

    ring_landed(count + part - 1)
    passage_grad_chunk(part - 1, True)
    passage_grad_chunk(count - 1, False)
    lax.fori_loop(count + part - 2, count + part, finish_ring, 0)


PIECES = 4


def write_kernel(loss, query_grad, passage_grad, loss_ref, query_grad_hbm, passage_grad_hbm, sem):
    loss_ref[...] = loss[0:1, 0:1]
    size = query_grad.shape[0] // PIECES
    copies = []
    for i, (source, target) in enumerate([(query_grad, query_grad_hbm), (passage_grad, passage_grad_hbm)]):
        for piece in range(PIECES):
            here = pl.ds(piece * size, size)
            copies.append(pltpu.make_async_copy(source.at[here], target.at[here], sem.at[i, piece]))
    for copy in copies:
        copy.start()
    for copy in copies:
        copy.wait()


def write_out(loss, query_grad, passage_grad):
    vmem, anywhere = pl.BlockSpec(memory_space=pltpu.VMEM), pl.BlockSpec(memory_space=pltpu.HBM)
    loss, query_grad, passage_grad = pl.pallas_call(
        write_kernel,
        out_shape=[
            jax.ShapeDtypeStruct((1, 1), jnp.float32),
            jax.ShapeDtypeStruct(query_grad.shape, jnp.float32),
            jax.ShapeDtypeStruct(passage_grad.shape, jnp.float32),
        ],
        in_specs=[vmem, vmem, vmem],
        out_specs=[vmem, anywhere, anywhere],
        scratch_shapes=[pltpu.SemaphoreType.DMA((2, PIECES))],
        compiler_params=pltpu.CompilerParams(vmem_limit_bytes=2**20),
    )(*[pltpu.with_memory_space_constraint(a, pltpu.VMEM) for a in (loss, query_grad, passage_grad)])
    return loss[0, 0], query_grad, passage_grad


def shards(queries, passages, cluster_of_block, positive_row, query_weight):
    rows, width = queries.shape
    count = width // CHUNK
    dma = pltpu.SemaphoreType.DMA
    vmem = pltpu.VMEM
    low, full = jnp.bfloat16, jnp.float32
    tile = (8, 128)
    slots = count + count // 2
    scratch = [
        pltpu.SMEM(cluster_of_block.shape, jnp.int32),
        vmem((rows // 128, 128), jnp.int32),
        vmem((rows // 128, 128), full),
        vmem((2 * count, rows, CHUNK), full),
        vmem((2 * count, rows, CHUNK), low),
        vmem((2, 2 * count, rows, CHUNK), low),
        vmem((NY - 1, count, rows, CHUNK), low),
        vmem((NY - 1, count, rows, CHUNK), low),
        vmem((NY - 1, rows, CHUNK), low),
        vmem((NY - 1, rows, CHUNK), low),
        vmem((2, count // 2, rows, CHUNK), low),
        vmem((2, count // 2, rows, CHUNK), low),
        vmem((2, slots, rows, CHUNK), low),
        vmem((2, slots, rows, CHUNK), low),
        vmem((2, count // 2 + EASY, rows, CHUNK), low),
        vmem((rows, NY * rows), full),
        vmem((rows // 2, NY * rows), full),
        vmem((NY, rows, rows), low),
        vmem((NY - 1, rows // 2, rows), low),
        vmem((NY - 1, rows // 2, rows), low),
        vmem((NY + 1, rows // 2, rows), low),
        vmem((NY + 1, rows // 2, rows), low),
        vmem((NY + 1, rows // 2, rows), low),
        vmem((NY, rows, rows), low),
        vmem((NY, rows, rows), low),
        vmem((rows, 128), full),
        vmem((rows, 128), full),
        vmem(tile, full),
        vmem((2,) + tile, full),
        vmem((NY,) + tile, full),
        vmem((NZ,) + tile, full),
        vmem((NX,) + tile, full),
        dma((2 * count,)),
        dma((2, 2 * count)),
        dma((2, 2 * count)),
        dma((NY - 1, count)),
        dma((NY - 1, count)),
        dma, dma,
        dma((NY - 1,)), dma((NY - 1,)),
        dma((NY - 1,)), dma((NY - 1,)),
        dma((3,)), dma((3,)),
        dma((NY,)), dma((NY,)),
        dma((NZ,)), dma((NZ,)),
        dma((NX,)), dma((NX,)),
        dma((NY - 1,)), dma((NY - 1,)),
        dma((3,)),
        dma((2, slots)), dma((2, slots)),
        dma((2, count // 2)), dma((2, count // 2)),
        dma((2, count // 2 + EASY)), dma((2, count // 2 + EASY)),
        dma, dma,
        dma, dma((2,)),
    ]
    in_vmem = pl.BlockSpec(memory_space=pltpu.VMEM)
    loss, query_grad, passage_grad = pl.pallas_call(
        kernel,
        out_shape=[
            jax.ShapeDtypeStruct(tile, full),
            vmem((rows, width), full),
            vmem((rows, width), full),
        ],
        in_specs=[pl.BlockSpec(memory_space=pltpu.HBM)] * 5,
        out_specs=[in_vmem, in_vmem, in_vmem],
        scratch_shapes=scratch,
        compiler_params=pltpu.CompilerParams(
            collective_id=0, has_side_effects=True, vmem_limit_bytes=36 * 2**20
        ),
        cost_estimate=pl.CostEstimate(
            flops=6 * NY * rows * rows * width, bytes_accessed=16 * rows * width, transcendentals=NY * rows * rows
        ),
    )(
        *[
            pltpu.with_memory_space_constraint(array, pltpu.HBM)
            for array in (
                queries, passages, cluster_of_block,
                positive_row.reshape(rows // 128, 128), query_weight.reshape(rows // 128, 128),
            )
        ]
    )
    return write_out(loss, query_grad, passage_grad)


def solution(mesh):
    in_specs = (P("dp", "mp"), P("dp", "mp"), P(), P("dp"), P("dp"))
    out_specs = (P(), P("dp", "mp"), P("dp", "mp"))
    return jax.shard_map(shards, mesh=mesh, in_specs=in_specs, out_specs=out_specs, check_vma=False)
```

```python
import functools
import math

import jax
import jax.numpy as jnp
from jax import lax
from jax.experimental import pallas as pl
from jax.experimental.pallas import tpu as pltpu
from jax.sharding import PartitionSpec as P

MESH = pl.DeviceIdType.MESH
NY, NZ, NX = 4, 8, 4
CHUNK = 256
GROUP = 32
EASY = 1


def nt_dot(left, right):
    return lax.dot_general(left, right, (((1,), (1,)), ((), ())), preferred_element_type=jnp.float32)


def nn_dot(left, right):
    return jnp.dot(left, right, preferred_element_type=jnp.float32)


def kernel(
    query_hbm, passage_hbm, cluster_hbm, positive_hbm, weight_hbm,
    loss_ref, query_grad, passage_grad,
    cluster, positive, weight, fresh, own, beside, staged, gathered, raw, raw_beside,
    passed, across, ring_out, ring_in, late_in,
    score_own, score_other, coeff, coeff_out, coeff_beside, coeff_staged, coeff_got, coeff_fwd, coeff_t, middle_t,
    pos_cols, weight_cols, loss_tile, loss_core, loss_y, loss_z, loss_x,
    in_sem, z_send, z_recv, y_send, y_recv, s_send, s_recv,
    cz_send, cz_recv, cy_send, cy_recv, cf_send, cf_recv,
    ly_send, ly_recv, lz_send, lz_recv, lx_send, lx_recv, raw_send, raw_recv, small_sem, ring_send, ring_recv, hop_send, hop_recv,
    late_send, late_recv, ch_send, ch_recv, lc_send, lc_recv,
):
    rows, width = query_hbm.shape
    count = width // CHUNK
    half = rows // 2
    planes = NX * NZ
    me = lax.axis_index("dp")
    core = lax.axis_index("mp")
    y = me % NY
    plane = me // NY
    z = plane % NZ
    x = plane // NZ

    def at_y(step):
        return plane * NY + (y + step) % NY

    def at_z(step):
        return (x * NZ + (z + step) % NZ) * NY + y

    def at_x(step):
        return (((x + step) % NX) * NZ + z) * NY + y

    left_plane = ((plane + planes - 1) % planes) * NY + y
    right_plane = ((plane + 1) % planes) * NY + y
    one_way = [jnp.where(y + s < NY, right_plane, left_plane) for s in range(1, NY)]
    other_way = [jnp.where(y + s < NY, left_plane, right_plane) for s in range(1, NY)]

    def arriving(k):
        start = pl.multiple_of(k * CHUNK, CHUNK)
        return pltpu.make_async_copy(passage_hbm.at[:, pl.ds(start, CHUNK)], fresh.at[k], in_sem.at[k])

    def arriving_query(k):
        start = pl.multiple_of(k * CHUNK, CHUNK)
        return pltpu.make_async_copy(
            query_hbm.at[:, pl.ds(start, CHUNK)], fresh.at[count + k], in_sem.at[count + k]
        )

    def start_in(k, carry):
        arriving(k).start()
        return carry

    def start_in_query(k, carry):
        arriving_query(k).start()
        return carry

    small = [
        pltpu.make_async_copy(source, target, small_sem.at[i])
        for i, (source, target) in enumerate(
            [(cluster_hbm, cluster), (positive_hbm, positive), (weight_hbm, weight)]
        )
    ]
    arriving(0).start()
    for copy in small:
        copy.start()
    lax.fori_loop(1, count, start_in, 0)
    lax.fori_loop(0, count, start_in_query, 0)

    barrier = pltpu.get_barrier_semaphore()
    peers = [at_y(s) for s in range(1, NY)] + [at_z(s) for s in range(1, NZ)] + [at_x(s) for s in range(1, NX)]
    peers = peers + [left_plane, right_plane]
    for peer in peers:
        pl.semaphore_signal(barrier, inc=1, device_id=(peer, core), device_id_type=MESH)
    pl.semaphore_signal(barrier, inc=1, device_id=(me, 1 - core), device_id_type=MESH)
    for copy in small:
        copy.wait()

    last = planes * NY - 1
    mine = cluster[me]
    on_left = cluster[jnp.maximum(me - NY, 0)]
    on_right = cluster[jnp.minimum(me + NY, last)]
    has_left = plane > 0
    has_right = plane < planes - 1
    want_left, want_right, linked = [], [], [None]
    got_beside = [None]
    for step in range(1, NY):
        target = at_y(step)
        theirs = cluster[target]
        want_left.append(has_left & (theirs == on_left))
        want_right.append(has_right & (theirs == on_right))
        from_here = theirs == mine
        from_left = has_left & (cluster[jnp.maximum(target - NY, 0)] == mine)
        from_right = has_right & (cluster[jnp.minimum(target + NY, last)] == mine)
        linked.append(from_here | from_left | from_right)
        got_beside.append(from_left | from_right)

    def same(step):
        there = me + step
        inside = (there >= 0) & (there <= last)
        return inside & (cluster[jnp.clip(there, 0, last)] == mine)

    near_up, near_down = same(1), same(-1)
    far_up, far_down = same(2), same(-2)
    middle = near_up & near_down & jnp.logical_not(far_up) & jnp.logical_not(far_down)
    top_end = near_down & far_down & jnp.logical_not(same(-3)) & jnp.logical_not(near_up)
    low_end = near_up & far_up & jnp.logical_not(same(3)) & jnp.logical_not(near_down)
    from_beside = [want_left[0] | want_right[0], want_left[2] | want_right[2]]

    def pick(step, here, from_left, from_right):
        return lax.select(
            want_left[step - 1], from_left, lax.select(want_right[step - 1], from_right, here)
        )

    def send(source, target, send_sem, recv_sem, place, where=None):
        return pltpu.make_async_remote_copy(
            src_ref=source, dst_ref=target, send_sem=send_sem, recv_sem=recv_sem,
            device_id=(place, core if where is None else where), device_id_type=MESH,
        )

    def along_z(k):
        return [
            send(own.at[k], beside.at[0, k], z_send.at[0, k], z_recv.at[0, k], right_plane),
            send(own.at[k], beside.at[1, k], z_send.at[1, k], z_recv.at[1, k], left_plane),
        ]

    def along_y(k):
        return [
            send(
                staged.at[s - 1, k], gathered.at[NY - s - 1, k],
                y_send.at[s - 1, k], y_recv.at[NY - s - 1, k], at_y(s),
            )
            for s in range(1, NY)
        ]

    def share(k):
        for copy in along_z(k):
            copy.start()

    def relay(k):
        for copy in along_z(k):
            copy.wait_recv()
        here, from_left, from_right = own[k], beside[0, k], beside[1, k]
        for s in range(1, NY):
            staged[s - 1, k] = pick(s, here, from_left, from_right)
        for copy in along_y(k):
            copy.start()

    def landed(k):
        for copy in along_y(k):
            copy.wait_recv()

    def block(k, slot):
        return own[k] if slot == 0 else gathered[slot - 1, k]

    def add_scores(k, first=False):
        mine_now = own[count + k]
        for slot in range(NY):
            columns = slice(slot * rows, (slot + 1) * rows)
            part = nt_dot(mine_now, block(k, slot))
            if first:
                score_own[:, columns] = part
            else:
                score_own[:, columns] += part

    def cast_passage(k):
        arriving(k).wait()
        own[k] = fresh[k].astype(jnp.bfloat16)

    def first_along_y():
        return [
            send(own.at[0], raw.at[NY - s - 1], y_send.at[s - 1, 0], y_recv.at[NY - s - 1, 0], at_y(s))
            for s in range(1, NY)
        ]

    def first_along_z():
        return [
            send(raw.at[s - 1], raw_beside.at[s - 1], raw_send.at[s - 1], raw_recv.at[s - 1], one_way[s - 1])
            for s in range(1, NY)
        ]

    cast_passage(0)
    pl.semaphore_wait(barrier, len(peers) + 1)
    for copy in first_along_y():
        copy.start()
    for k in range(1, 4):
        cast_passage(k)
        share(k)

    def cast_rest(k, carry):
        cast_passage(k)
        return carry

    def cast_queries(k, carry):
        arriving_query(k).wait()
        own[count + k] = fresh[count + k].astype(jnp.bfloat16)
        return carry

    lax.fori_loop(4, count, cast_rest, 0)
    lax.fori_loop(0, count, cast_queries, 0)

    for part in range(rows // 128):
        here = slice(part * 128, (part + 1) * 128)
        as_row = positive[part : part + 1, :].astype(jnp.float32)
        pos_cols[here, :] = jnp.broadcast_to(as_row, (128, 128)).T
        weight_cols[here, :] = jnp.broadcast_to(weight[part : part + 1, :], (128, 128)).T

    relay(1)
    share(4)
    for copy in first_along_y():
        copy.wait_recv()
    relay(2)
    share(5)
    landed(1)
    add_scores(1, first=True)

    part = count // 2
    hop_place = [
        jnp.where(y == NY - 1, right_plane, left_plane),
        jnp.where(y == 0, left_plane, right_plane),
    ]
    wraps = [y == NY - 1, y == 0]
    steps = [1, NY - 1]

    def ring(way, q):
        return send(
            ring_out.at[way, q], ring_in.at[way, q], ring_send.at[way, q], ring_recv.at[way, q], at_y(steps[way])
        )

    def hop(way, j, relayed=False):
        source = ring_in.at[way, j] if relayed else passed.at[way, j]
        return send(source, across.at[way, j], hop_send.at[way, j], hop_recv.at[way, j], hop_place[way])

    late_place = [right_plane, left_plane]
    late_columns = [y == 0, y == NY - 1]
    late_wanted = [near_down, near_up]

    def late(way, j):
        return send(
            ring_in.at[way, part + j], late_in.at[way, j], late_send.at[way, j], late_recv.at[way, j], late_place[way]
        )

    def query_chunk(way, q):
        return count + (q + part) % count if way == 0 else count + q

    def ring_first(q):
        for k in (q, q + part):
            for copy in along_z(count + k):
                copy.wait_recv()
        for way in range(2):
            k = query_chunk(way, q)
            ring_out[way, q] = pick(steps[way], own[k], beside[0, k], beside[1, k])
            ring(way, q).start()

    def ring_landed(q):
        for way in range(2):
            ring(way, q).wait_recv()

    def pass_relayed(j):
        for way in range(2):

            @pl.when(jnp.logical_not(wraps[way]))
            def _():
                hop(way, j, True).start()

    def ring_second(j):
        q = part + j
        for way in range(2):
            k = query_chunk(way, q)
            here = lax.select(middle, ring_in[way, j], own[k])
            s = steps[way] - 1
            inside = jnp.logical_not(wraps[way])
            here = lax.select(inside & want_right[s], beside[1, k], here)
            ring_out[way, q] = lax.select(inside & want_left[s], beside[0, k], here)
            ring(way, q).start()

    def last_content(way, j):
        k = query_chunk(way, part + j)
        terms = nn_dot(middle_t[way], own[k]) + nn_dot(middle_t[2 + way], ring_in[way, part + j])
        passed[way, j] = lax.select(middle, terms.astype(jnp.bfloat16), ring_in[way, j])

    def start_late(j):
        for way in range(2):

            @pl.when(late_columns[way])
            def _():
                late(way, j).start()

    def finish_late(j):
        for way in range(2):

            @pl.when(late_columns[way])
            def _():
                late(way, j).wait()
                ring_in[way, part + j] = lax.select(late_wanted[way], late_in[way, j], ring_in[way, part + j])

    def begin_last(j):
        for way in range(2):

            @pl.when(wraps[way])
            def _():
                last_content(way, j)
                if j >= EASY:
                    hop(way, j).start()

    def finish_last(j):
        finish_late(j)
        for way in range(2):

            @pl.when(jnp.logical_not(wraps[way]))
            def _():
                last_content(way, j)

    def ring_last(j):
        q = count + j
        for way in range(2):
            if j >= EASY:
                hop(way, j).wait_recv()
                ring_out[way, q] = lax.select(from_beside[way], across[way, j], passed[way, j])
            else:

                @pl.when(wraps[way])
                def _():
                    ring_out[way, q] = passed[way, j]

                @pl.when(jnp.logical_not(wraps[way]))
                def _():
                    hop(way, j).wait_recv()
                    ring_out[way, q] = lax.select(from_beside[way], across[way, j], passed[way, j])

            ring(way, q).start()

    def passage_step(k, shares):
        relay(k)
        for share_now in shares:
            share(share_now)
        landed(k - 1)
        add_scores(k - 1)

    passage_step(3, [6])
    for copy in first_along_z():
        copy.start()
    passage_step(4, [7])
    for k in range(5, count):
        passage_step(k, [count + k - 5, count + part + k - 5])
    for copy in first_along_z():
        copy.wait_recv()
    for slot in range(1, NY):
        gathered[slot - 1, 0] = lax.select(got_beside[slot], raw_beside[slot - 1], raw[slot - 1])
    add_scores(0)
    share(count + part - 1)
    share(2 * count - 1)
    ring_first(0)
    landed(count - 1)
    ring_first(1)
    add_scores(count - 1)
    my_half = pl.ds(pl.multiple_of(core * half, half), half)
    their_half = pl.ds(pl.multiple_of((1 - core) * half, half), half)
    swap = send(score_own.at[their_half], score_other, s_send, s_recv, me, 1 - core)
    swap.start()
    ring_first(2)
    swap.wait_recv()

    scale = 3.0 / math.sqrt(2 * width)

    def soft_rows(group, total):
        here = pl.ds(pl.multiple_of(core * half + group * GROUP, GROUP), GROUP)
        there = pl.ds(pl.multiple_of(group * GROUP, GROUP), GROUP)
        tiles = []
        for slot in range(NY):
            columns = slice(slot * rows, (slot + 1) * rows)
            tile = (score_own[here, columns] + score_other[there, columns]) * scale
            if slot > 0:
                tile = lax.select(linked[slot], tile, jnp.full_like(tile, -1e30))
            tiles.append(tile)
        top = functools.reduce(jnp.maximum, [jnp.max(t, axis=1, keepdims=True) for t in tiles])
        expo = [jnp.exp(t - top) for t in tiles]
        row_total = functools.reduce(jnp.add, [jnp.sum(e, axis=1, keepdims=True) for e in expo])
        wanted = pos_cols[here, 0:1]
        heavy = weight_cols[here, 0:1]
        columns = lax.broadcasted_iota(jnp.int32, (GROUP, rows), 1).astype(jnp.float32)
        hit = columns == wanted
        picked = jnp.sum(jnp.where(hit, tiles[0], 0.0), axis=1, keepdims=True)
        ratio = heavy / row_total
        for slot in range(NY):
            value = expo[slot] * ratio
            if slot == 0:
                value = value - jnp.where(hit, heavy, 0.0)
            coeff[slot, here, :] = value.astype(jnp.bfloat16)
        return total + heavy * (top + jnp.log(row_total) - picked)

    total = lax.fori_loop(0, half // GROUP, soft_rows, jnp.zeros((GROUP, 1), jnp.float32))
    for s in range(1, NY):
        coeff_out[s - 1] = coeff[s, my_half, :]
    coeff_z = [
        send(coeff_out.at[s - 1], coeff_beside.at[s - 1], cz_send.at[s - 1], cz_recv.at[s - 1], other_way[s - 1])
        for s in range(1, NY)
    ]
    for copy in coeff_z:
        copy.start()

    halves = send(coeff.at[:, my_half, :], coeff.at[:, my_half, :], ch_send, ch_recv, me, 1 - core)
    halves.start()
    loss_core[core] = jnp.broadcast_to(jnp.sum(total, axis=0, keepdims=True), loss_tile.shape)
    loss_across = send(loss_core.at[core], loss_core.at[core], lc_send, lc_recv.at[core], me, 1 - core)
    loss_across.start()

    def spread(buffer, send_sem, recv_sem, mine_at, size, place):
        return [
            send(loss_tile, buffer.at[mine_at], send_sem.at[s - 1], recv_sem.at[mine_at], place(s))
            for s in range(1, size)
        ]

    def collect(buffer, recv_sem, mine_at, size):
        buffer[mine_at] = loss_tile[...]
        for s in range(1, size):
            source = (mine_at + s) % size
            send(loss_tile, buffer.at[source], recv_sem.at[source], recv_sem.at[source], me, 1 - core).wait_recv()
        value = buffer[0]
        for s in range(1, size):
            value = value + buffer[s]
        return value

    ring_first(3)
    ring_landed(0)
    ring_landed(1)
    halves.wait_recv()

    def query_grad_step(k, carry):
        value = nn_dot(coeff[0], own[k])
        for slot in range(1, NY):
            value = value + nn_dot(coeff[slot], gathered[slot - 1, k])
        query_grad[:, pl.ds(pl.multiple_of(k * CHUNK, CHUNK), CHUNK)] = value
        return carry


    send(
        loss_core.at[1 - core], loss_core.at[1 - core], lc_send, lc_recv.at[1 - core], me, 1 - core
    ).wait_recv()
    loss_tile[...] = loss_core[0] + loss_core[1]
    loss_along_y = spread(loss_y, ly_send, ly_recv, y, NY, at_y)
    for copy in loss_along_y:
        copy.start()

    for copy in coeff_z:
        copy.wait_recv()
    for place, (s, tile) in enumerate([(1, 1), (1, 2), (2, 2), (3, 3), (3, 2)]):
        coeff_staged[place] = lax.select(
            want_left[s - 1] | want_right[s - 1], coeff_beside[tile - 1], coeff_out[tile - 1]
        )
    coeff_y = [
        send(coeff_staged.at[0:2], coeff_got.at[3:5], cy_send.at[0], cy_recv.at[2], at_y(1)),
        send(coeff_staged.at[2], coeff_got.at[2], cy_send.at[1], cy_recv.at[1], at_y(2)),
        send(coeff_staged.at[3:5], coeff_got.at[0:2], cy_send.at[2], cy_recv.at[0], at_y(3)),
    ]
    for message in (0, 2, 1):
        coeff_y[message].start()

    ring_second(0)
    pass_relayed(0)
    pass_relayed(1)
    ring_landed(2)
    pass_relayed(2)
    ring_second(1)
    lax.fori_loop(0, count, query_grad_step, 0)
    ring_landed(3)
    pass_relayed(3)
    value = collect(loss_y, ly_recv, y, NY)
    for copy in loss_along_y:
        copy.wait_send()
    loss_tile[...] = value
    loss_along_z = spread(loss_z, lz_send, lz_recv, z, NZ, at_z)
    for copy in loss_along_z:
        copy.start()
    ring_second(2)
    coeff_y[0].wait_recv()
    coeff_y[2].wait_recv()
    forward = [
        send(coeff_got.at[piece], coeff_fwd.at[piece], cf_send.at[i], cf_recv.at[i], me, 1 - core)
        for i, piece in enumerate((slice(0, 2), slice(2, 3), slice(3, 5)))
    ]
    forward[0].start()
    forward[2].start()
    ring_second(3)

    def turned(tile):
        return tile.astype(jnp.float32).T

    coeff_t[0] = turned(coeff[0]).astype(jnp.bfloat16)
    middle_t[0] = turned(coeff[1]).astype(jnp.bfloat16)
    middle_t[1] = turned(coeff[3]).astype(jnp.bfloat16)
    ring_landed(4)
    start_late(0)
    forward[0].wait_recv()
    forward[2].wait_recv()
    first_half = core == 0

    def whole(place):
        got, fwd = coeff_got[place], coeff_fwd[place]
        return turned(
            jnp.concatenate([lax.select(first_half, got, fwd), lax.select(first_half, fwd, got)], axis=0)
        )

    middle_t[2] = whole(4).astype(jnp.bfloat16)
    middle_t[3] = whole(1).astype(jnp.bfloat16)
    begin_last(0)
    coeff_y[1].wait_recv()
    forward[1].start()
    ring_landed(5)
    start_late(1)
    begin_last(1)
    finish_last(0)
    ring_last(0)
    forward[1].wait_recv()
    for slot, place in ((1, 0), (2, 2), (3, 3)):
        tile = whole(place)
        coeff_t[slot] = lax.select(linked[slot], tile, jnp.zeros_like(tile)).astype(jnp.bfloat16)
    ring_landed(6)
    start_late(2)
    begin_last(2)
    finish_last(1)
    ring_last(1)
    ring_landed(7)
    start_late(3)
    begin_last(3)
    finish_last(2)
    ring_last(2)
    value = collect(loss_z, lz_recv, z, NZ)
    for copy in loss_along_z:
        copy.wait_send()
    loss_tile[...] = value
    loss_along_x = spread(loss_x, lx_send, lx_recv, x, NX, at_x)
    for copy in loss_along_x:
        copy.start()
    finish_last(3)
    ring_last(3)

    def passage_grad_chunk(k, start):
        j = k % part
        up, down = ring_in[0, (k + part) % count], ring_in[1, k]
        far = ring_in[1 if start else 0, count + j]
        relayed = ring_in[1 if start else 0, part + j]
        near_end, far_end = (low_end, top_end) if start else (top_end, low_end)
        done = ring_in[0 if start else 1, count + j].astype(jnp.float32)
        from_up = nn_dot(coeff_t[NY - 1], up)
        from_down = nn_dot(coeff_t[1], down)
        if start:
            from_up = lax.select(far_end, done, from_up)
        else:
            from_down = lax.select(far_end, done, from_down)
        opposite = nn_dot(coeff_t[2], lax.select(near_end, relayed, far))
        opposite = lax.select(far_end, jnp.zeros_like(opposite), opposite)
        value = nn_dot(coeff_t[0], own[count + k]) + from_up + from_down + opposite
        passage_grad[:, k * CHUNK : (k + 1) * CHUNK] = value

    for j in range(EASY):
        ring_landed(count + j)
        start_late(part + j)
    value = collect(loss_x, lx_recv, x, NX)
    for copy in loss_along_x:
        copy.wait_send()
    loss_ref[...] = value * (1.0 / (rows * planes * NY))
    for j in range(EASY, part - 1):
        ring_landed(count + j)
        if j == EASY:
            for i in range(EASY):
                finish_late(part + i)
                passage_grad_chunk(i, True)
                passage_grad_chunk(part + i, False)
        passage_grad_chunk(j, True)
        passage_grad_chunk(part + j, False)

    def finish_shares(k, carry):
        for copy in along_z(k):
            copy.wait_send()
        return carry

    def finish_chunks(k, carry):
        for copy in along_y(k):
            copy.wait_send()
        return carry

    def finish_ring(q, carry):
        for way in range(2):
            ring(way, q).wait_send()
        return carry

    def finish_hops(j, carry):
        for way in range(2):
            hop(way, j).wait_send()
        return carry

    lax.fori_loop(1, 2 * count, finish_shares, 0)
    lax.fori_loop(1, count, finish_chunks, 0)
    lax.fori_loop(0, count + part - 2, finish_ring, 0)
    for way in range(2):

        @pl.when(jnp.logical_not(wraps[way]))
        def _():
            for j in range(EASY):
                hop(way, j).wait_send()

    lax.fori_loop(EASY, part, finish_hops, 0)
    for copy in first_along_y() + first_along_z() + coeff_z + coeff_y + forward + [swap, halves, loss_across]:
        copy.wait_send()

    ring_landed(count + part - 1)
    passage_grad_chunk(part - 1, True)
    passage_grad_chunk(count - 1, False)
    lax.fori_loop(count + part - 2, count + part, finish_ring, 0)


PIECES = 4


def write_kernel(loss, query_grad, passage_grad, loss_ref, query_grad_hbm, passage_grad_hbm, sem):
    loss_ref[...] = loss[0:1, 0:1]
    size = query_grad.shape[0] // PIECES
    copies = []
    for i, (source, target) in enumerate([(query_grad, query_grad_hbm), (passage_grad, passage_grad_hbm)]):
        for piece in range(PIECES):
            here = pl.ds(piece * size, size)
            copies.append(pltpu.make_async_copy(source.at[here], target.at[here], sem.at[i, piece]))
    for copy in copies:
        copy.start()
    for copy in copies:
        copy.wait()


def write_out(loss, query_grad, passage_grad):
    vmem, anywhere = pl.BlockSpec(memory_space=pltpu.VMEM), pl.BlockSpec(memory_space=pltpu.HBM)
    loss, query_grad, passage_grad = pl.pallas_call(
        write_kernel,
        out_shape=[
            jax.ShapeDtypeStruct((1, 1), jnp.float32),
            jax.ShapeDtypeStruct(query_grad.shape, jnp.float32),
            jax.ShapeDtypeStruct(passage_grad.shape, jnp.float32),
        ],
        in_specs=[vmem, vmem, vmem],
        out_specs=[vmem, anywhere, anywhere],
        scratch_shapes=[pltpu.SemaphoreType.DMA((2, PIECES))],
        compiler_params=pltpu.CompilerParams(vmem_limit_bytes=2**20),
    )(*[pltpu.with_memory_space_constraint(a, pltpu.VMEM) for a in (loss, query_grad, passage_grad)])
    return loss[0, 0], query_grad, passage_grad


def shards(queries, passages, cluster_of_block, positive_row, query_weight):
    rows, width = queries.shape
    count = width // CHUNK
    dma = pltpu.SemaphoreType.DMA
    vmem = pltpu.VMEM
    low, full = jnp.bfloat16, jnp.float32
    tile = (8, 128)
    slots = count + count // 2
    scratch = [
        pltpu.SMEM(cluster_of_block.shape, jnp.int32),
        vmem((rows // 128, 128), jnp.int32),
        vmem((rows // 128, 128), full),
        vmem((2 * count, rows, CHUNK), full),
        vmem((2 * count, rows, CHUNK), low),
        vmem((2, 2 * count, rows, CHUNK), low),
        vmem((NY - 1, count, rows, CHUNK), low),
        vmem((NY - 1, count, rows, CHUNK), low),
        vmem((NY - 1, rows, CHUNK), low),
        vmem((NY - 1, rows, CHUNK), low),
        vmem((2, count // 2, rows, CHUNK), low),
        vmem((2, count // 2, rows, CHUNK), low),
        vmem((2, slots, rows, CHUNK), low),
        vmem((2, slots, rows, CHUNK), low),
        vmem((2, count // 2 + EASY, rows, CHUNK), low),
        vmem((rows, NY * rows), full),
        vmem((rows // 2, NY * rows), full),
        vmem((NY, rows, rows), low),
        vmem((NY - 1, rows // 2, rows), low),
        vmem((NY - 1, rows // 2, rows), low),
        vmem((NY + 1, rows // 2, rows), low),
        vmem((NY + 1, rows // 2, rows), low),
        vmem((NY + 1, rows // 2, rows), low),
        vmem((NY, rows, rows), low),
        vmem((NY, rows, rows), low),
        vmem((rows, 128), full),
        vmem((rows, 128), full),
        vmem(tile, full),
        vmem((2,) + tile, full),
        vmem((NY,) + tile, full),
        vmem((NZ,) + tile, full),
        vmem((NX,) + tile, full),
        dma((2 * count,)),
        dma((2, 2 * count)),
        dma((2, 2 * count)),
        dma((NY - 1, count)),
        dma((NY - 1, count)),
        dma, dma,
        dma((NY - 1,)), dma((NY - 1,)),
        dma((NY - 1,)), dma((NY - 1,)),
        dma((3,)), dma((3,)),
        dma((NY,)), dma((NY,)),
        dma((NZ,)), dma((NZ,)),
        dma((NX,)), dma((NX,)),
        dma((NY - 1,)), dma((NY - 1,)),
        dma((3,)),
        dma((2, slots)), dma((2, slots)),
        dma((2, count // 2)), dma((2, count // 2)),
        dma((2, count // 2 + EASY)), dma((2, count // 2 + EASY)),
        dma, dma,
        dma, dma((2,)),
    ]
    in_vmem = pl.BlockSpec(memory_space=pltpu.VMEM)
    loss, query_grad, passage_grad = pl.pallas_call(
        kernel,
        out_shape=[
            jax.ShapeDtypeStruct(tile, full),
            vmem((rows, width), full),
            vmem((rows, width), full),
        ],
        in_specs=[pl.BlockSpec(memory_space=pltpu.HBM)] * 5,
        out_specs=[in_vmem, in_vmem, in_vmem],
        scratch_shapes=scratch,
        compiler_params=pltpu.CompilerParams(
            collective_id=0, has_side_effects=True, vmem_limit_bytes=36 * 2**20
        ),
        cost_estimate=pl.CostEstimate(
            flops=6 * NY * rows * rows * width, bytes_accessed=16 * rows * width, transcendentals=NY * rows * rows
        ),
    )(
        *[
            pltpu.with_memory_space_constraint(array, pltpu.HBM)
            for array in (
                queries, passages, cluster_of_block,
                positive_row.reshape(rows // 128, 128), query_weight.reshape(rows // 128, 128),
            )
        ]
    )
    return write_out(loss, query_grad, passage_grad)


def solution(mesh):
    in_specs = (P("dp", "mp"), P("dp", "mp"), P(), P("dp"), P("dp"))
    out_specs = (P(), P("dp", "mp"), P("dp", "mp"))
    return jax.shard_map(shards, mesh=mesh, in_specs=in_specs, out_specs=out_specs, check_vma=False)
```
